128 devices in a mesh: row: 8 (over z, core), col: 16 (over x, y).
Axes of the slice: x: 4, y: 4, z: 4, core: 2. Of those that a mesh axis runs over, the one named last changes fastest.
Arguments:
- form_rows: bfloat16 [4096, 64, 512], P(('row', 'col')), may hold values from -6 to 6
- form_strip: bfloat16 [16, 64, 512], P('col'), may hold values from -0.25 to 0.25
- lam_index: int32 [4096, 16, 8], P(('row', 'col')), may hold values from 0 to 15
- coef_index: int32 [4096, 16, 8], P(('row', 'col')), may hold values from 0 to 63
- term_count: int32 [4096, 16], P(('row', 'col')), may hold values from 1 to 8
- angular_coef: float32 [64], replicated, may hold values from -3 to 3
- kernels: float32 [16, 512], replicated, may hold values from 0.1 to 2
- pivots: int32 [512], replicated, may hold values from 0 to 262143, as said below
- lower_inverse: float32 [512, 512], replicated, as said below
- panel: bfloat16 [512, 262144], P('col', 'row'), may hold values from -0.25 to 0.25
Outputs:
- trailing: float32 [1024, 262144], P('col', 'row')
- upper_rows: bfloat16 [1024, 512], P('col')
The draws below stay inside these ranges and needn't reach their ends.
Inputs may be any that keep to these rules, and one draw needn't show every extreme that they name: pivots are distinct strip rows; row 0 and row 262143 are always among them. lower_inverse is unit lower triangular.
All inputs are finite; a program needn't handle non-finite values.
Results may differ from the reference program's by a relative error of at most 0.0057.
Values may be sent and summed in bfloat16 or wider, within the bound.
No kernel may reach another device: no remote copies, remote signals or barrier semaphores. Data moves between devices by JAX's collectives and lax.ppermute only.
A program may use at most 192 MiB of HBM per device.

```python
import math
import jax
import jax.numpy as jnp
from jax import lax

NK = 64
NR = 512
SCH = 16
NLAM = 16
NCOEF = 64
TERMS = 8
NPIV = 512
RCH = 4096
ROWS = 262144
N_ROW = 8


def draw_pivots(key, part):
    key = jax.random.fold_in(key, 11)
    inner = jax.random.permutation(key, RCH * NK - 2)[:NPIV - 2] + 1
    rows_all = jnp.concatenate([jnp.array([0, RCH * NK - 1], dtype=jnp.int32), inner.astype(jnp.int32)])
    order = jax.random.permutation(jax.random.fold_in(key, 5), NPIV)
    return jnp.take(rows_all, order).astype(jnp.int32)


def draw_lower_inverse(key, part):
    key = jax.random.fold_in(key, 23)
    values = jax.random.normal(key, (NPIV, NPIV), jnp.float32)
    lower = jnp.tril(values * (0.8 / NPIV ** 0.5), -1)
    return (lower + jnp.eye(NPIV, dtype=jnp.float32)).astype(jnp.float32)


def touch_ends(entries, stream_key, least, largest):
    shape = entries.shape
    spot = [jax.random.randint(jax.random.fold_in(stream_key, axis), (), 0, shape[axis]) for axis in range(len(shape))]
    entries = entries.at[tuple(spot)].set(least)
    longest = shape.index(max(shape))
    spot[longest] = (spot[longest] + 1) % shape[longest]
    return entries.at[tuple(spot)].set(largest)


def block_levels(key, shape, shards, low, high):
    def one(dim, shards_of):
        steps = jax.random.uniform(jax.random.fold_in(jax.random.fold_in(key, 6), dim), (shards_of,), jnp.float32, low / len(shards), high / len(shards))
        return jnp.repeat(jnp.exp(steps), shape[dim] // shards_of).reshape((-1,) + (1,) * (len(shape) - dim - 1))

    factor_of = one(*shards[0])
    for cut in shards[1:]:
        factor_of = factor_of * one(*cut)
    return factor_of


def noise(rng, dims, spread, reach, cuts=(), held_as=jnp.bfloat16):
    drawn = jax.random.normal(rng, dims, jnp.float32) * spread
    if len(cuts) > 0:
        drawn = block_levels(rng, dims, cuts, -0.22, 0.18) * drawn
    return jnp.clip(drawn, min=-reach, max=reach).astype(held_as)


def setup_inputs(seed: int = 0) -> dict:
    splits = jax.random.split(jax.random.key(seed), 11)
    form_rows = noise(splits[0], (RCH, NK, NR), 1.0, 6.0, ((0, 128),))
    form_strip = noise(splits[1], (SCH, NK, NR), NR ** -0.5, 0.25, ((0, 16),))
    lam_index = touch_ends(jax.random.randint(splits[2], (RCH, SCH, TERMS), 0, NLAM), jax.random.fold_in(splits[2], 1), 0, NLAM - 1).astype(jnp.int32)
    coef_index = touch_ends(jax.random.randint(splits[3], (RCH, SCH, TERMS), 0, NCOEF), jax.random.fold_in(splits[3], 1), 0, NCOEF - 1).astype(jnp.int32)
    term_count = touch_ends(jax.random.randint(splits[4], (RCH, SCH), 1, TERMS + 1), jax.random.fold_in(splits[4], 1), 1, TERMS).astype(jnp.int32)
    angular_coef = noise(splits[5], (NCOEF,), 0.5, 3.0, (), jnp.float32)
    kernels = jnp.clip(jnp.exp(jax.random.uniform(splits[6], (NLAM, NR), jnp.float32, math.log(0.1), math.log(2.0))), 0.1, 2.0)
    pivots = draw_pivots(jax.random.fold_in(splits[10], 71), 0)
    lower_inverse = draw_lower_inverse(jax.random.fold_in(splits[10], 71), 0)
    panel = noise(splits[9], (NPIV, ROWS), NPIV ** -0.5, 0.25, ((0, 16), (1, 8)))
    return {"form_rows": form_rows, "form_strip": form_strip, "lam_index": lam_index, "coef_index": coef_index, "term_count": term_count, "angular_coef": angular_coef, "kernels": kernels, "pivots": pivots, "lower_inverse": lower_inverse, "panel": panel}


def term_weights(lam_index, coef_index, term_count, angular_coef, kernels):
    chans, strips, terms = lam_index.shape
    nlam = kernels.shape[0]
    ncoef = angular_coef.shape[0]
    position = lax.broadcasted_iota(jnp.int32, lam_index.shape, 2)
    live = (position < term_count[:, :, None]).astype(jnp.float32)
    coef_table = (coef_index[..., None] == jnp.arange(ncoef, dtype=jnp.int32)).astype(jnp.float32)
    coef_value = jnp.sum(coef_table * angular_coef, axis=-1)
    lam_table = (lam_index[..., None] == jnp.arange(nlam, dtype=jnp.int32)).astype(jnp.float32)
    mixing = jnp.sum((live * coef_value)[..., None] * lam_table, axis=2)
    radial = jnp.dot(mixing.reshape(chans * strips, nlam), kernels, precision=lax.Precision.HIGHEST)
    return radial.reshape(chans, strips, kernels.shape[1])


def reference(form_rows, form_strip, lam_index, coef_index, term_count, angular_coef, kernels, pivots, lower_inverse, panel):
    radial = term_weights(lam_index, coef_index, term_count, angular_coef, kernels)
    strip_f = form_strip.astype(jnp.float32)

    def assemble(pieces):
        rows_block, weight_block = pieces
        scaled = (rows_block.astype(jnp.float32)[:, None] * weight_block[:, :, None, :]).astype(jnp.bfloat16)
        blocks = jnp.einsum("ijkr,jlr->ikjl", scaled.astype(jnp.float32), strip_f)
        return blocks.astype(jnp.bfloat16)

    blocks = lax.map(assemble, (form_rows.reshape(RCH // 8, 8, NK, NR), radial.reshape(RCH // 8, 8, SCH, NR)))
    strip = blocks.reshape(RCH * NK, SCH * NK)
    chosen = jnp.take(strip, pivots, axis=0).astype(jnp.float32)
    upper = jnp.dot(lower_inverse, chosen, precision=lax.Precision.HIGHEST).astype(jnp.bfloat16)
    regrouped = strip.reshape(RCH // N_ROW, N_ROW, NK, SCH * NK).transpose(1, 0, 2, 3).reshape(RCH * NK, SCH * NK).T
    upper_rows = upper.T
    trailing = regrouped.astype(jnp.float32) - jnp.dot(upper_rows, panel, preferred_element_type=jnp.float32)
    return trailing, upper_rows
```

```python
import jax
import jax.numpy as jnp
from jax import lax
from jax.sharding import PartitionSpec as P

ALL = ("row", "col")


def exchange(chunks):
    return lax.all_to_all(chunks, ALL, split_axis=0, concat_axis=0, tiled=True)


def mixing_weights(lam, coef, angular_coef, nlam):
    coef_table = (coef[..., None] == jnp.arange(angular_coef.shape[0], dtype=coef.dtype)).astype(jnp.float32)
    coef_value = jnp.sum(coef_table * angular_coef, axis=-1)
    lam_table = (lam[..., None] == jnp.arange(nlam, dtype=lam.dtype)).astype(jnp.float32)
    return jnp.sum(coef_value[..., None] * lam_table, axis=-2)


def weights_to_radial(mixing, kernels):
    chans, strips, nlam = mixing.shape
    radial = jnp.dot(mixing.reshape(chans * strips, nlam), kernels, precision=lax.Precision.HIGHEST)
    return radial.reshape(chans, strips, kernels.shape[1])


def shards(
    form_rows,
    form_strip,
    lam_index,
    coef_index,
    term_count,
    angular_coef,
    kernels,
    pivots,
    lower_inverse,
    panel,
):
    nrow = lax.axis_size("row")
    ncol = lax.axis_size("col")
    ndev = nrow * ncol
    row = lax.axis_index("row")
    col = lax.axis_index("col")
    me = row * ncol + col
    chans, nmom, nrad = form_rows.shape
    nstrip, terms = lam_index.shape[1:]
    nlam = kernels.shape[0]
    npiv = pivots.shape[0]
    scols = nstrip * nmom
    width = scols // ncol
    own = npiv // ndev
    group = chans // nrow
    bf16, f32 = jnp.bfloat16, jnp.float32

    position = lax.broadcasted_iota(jnp.int32, lam_index.shape, 2)
    lam = jnp.where(position < term_count[:, :, None], lam_index, nlam)
    at_row = pivots - me * (chans * nmom)
    row_pick = (at_row[:, None] == jnp.arange(chans * nmom, dtype=jnp.int32)).astype(bf16)
    picked = jnp.dot(row_pick, form_rows.reshape(chans * nmom, nrad), preferred_element_type=f32)
    at_chan = pivots // nmom - me * chans
    chan_pick = (at_chan[:, None] == jnp.arange(chans, dtype=jnp.int32)).astype(bf16)
    term_table = jnp.concatenate([lam.reshape(chans, -1), coef_index.reshape(chans, -1)], axis=1).astype(bf16)
    picked_terms = jnp.dot(chan_pick, term_table, preferred_element_type=f32)
    share = nmom // nrow
    strip_share = lax.dynamic_slice_in_dim(form_strip[0], row * share, share, axis=0)
    first = jnp.concatenate(
        [
            picked.astype(bf16).reshape(ndev, own * nrad),
            picked_terms.astype(bf16).reshape(ndev, own * 2 * nstrip * terms),
            jnp.broadcast_to(strip_share.reshape(1, -1), (ndev, share * nrad)),
        ],
        axis=1,
    )
    lanes = 128
    got = exchange(first.reshape(ndev, -1, lanes)).reshape(ndev, -1)
    cut1 = own * nrad
    cut2 = cut1 + own * 2 * nstrip * terms
    my_rows = jnp.sum(got[:, :cut1].astype(f32), axis=0).reshape(own, nrad)
    my_terms = jnp.sum(got[:, cut1:cut2].astype(f32), axis=0).reshape(own, 2, nstrip, terms)
    strip_all = got[:, cut2:].reshape(nrow, ncol, share, nrad).transpose(1, 0, 2, 3).reshape(nstrip, nmom, nrad)

    my_mixing = mixing_weights(my_terms[:, 0].astype(jnp.int32), my_terms[:, 1].astype(jnp.int32), angular_coef, nlam)
    my_radial = weights_to_radial(my_mixing, kernels)
    my_scaled = (my_rows[:, None, :] * my_radial).astype(bf16)
    my_chosen = jnp.einsum("ajr,jlr->ajl", my_scaled, strip_all, preferred_element_type=f32).astype(bf16)

    panel_cut = panel.reshape(panel.shape[0], ndev, -1).transpose(1, 0, 2)
    deep, wide = panel_cut.shape[1:]
    second = jnp.concatenate(
        [panel_cut, jnp.broadcast_to(my_chosen.reshape(1, -1, wide), (ndev, own * scols // wide, wide))], axis=1
    )
    got2 = exchange(second)

    mixing = mixing_weights(lam, coef_index, angular_coef, nlam)
    radial = weights_to_radial(mixing, kernels)
    scaled = (form_rows.astype(f32)[:, None] * radial[:, :, None, :]).astype(bf16)
    scaled = scaled.reshape(group, nrow, nstrip, nmom, nrad)
    blocks = jnp.einsum("qpjkr,jlr->pjlqk", scaled, strip_all, preferred_element_type=f32).astype(bf16)
    blocks = blocks.reshape(nrow, scols, group * nmom)

    chosen = got2[:, deep:].reshape(npiv, scols)
    low1 = lower_inverse.astype(bf16)
    rest = lower_inverse - low1.astype(f32)
    low2 = rest.astype(bf16)
    low3 = (rest - low2.astype(f32)).astype(bf16)
    upper = (
        jnp.dot(low1, chosen, preferred_element_type=f32)
        + (jnp.dot(low2, chosen, preferred_element_type=f32) + jnp.dot(low3, chosen, preferred_element_type=f32))
    ).astype(bf16)
    columns = got2[:, :deep].reshape(nrow, npiv, wide)
    update = jnp.einsum("tn,ptm->pnm", upper, columns, preferred_element_type=f32)
    done = (blocks.astype(f32) - update).astype(bf16).reshape(ndev, width, wide)
    final = exchange(done)
    trailing = final.transpose(1, 0, 2).reshape(width, ndev * wide).astype(f32)
    upper_t = lax.dynamic_slice_in_dim(upper, col * width, width, axis=1).T
    return (trailing, upper_t)


def solution(mesh):
    in_specs = (
        P(("row", "col"), None, None),
        P("col", None, None),
        P(("row", "col"), None, None),
        P(("row", "col"), None, None),
        P(("row", "col"), None),
        P(),
        P(),
        P(),
        P(),
        P("col", "row"),
    )
    out_specs = (P("col", "row"), P("col", None))
    return jax.shard_map(shards, mesh=mesh, in_specs=in_specs, out_specs=out_specs, check_vma=False)
```

```python
import functools

import jax
import jax.numpy as jnp
from jax import lax
from jax.experimental import pallas as pl
from jax.experimental.pallas import tpu as pltpu
from jax.sharding import PartitionSpec as P

ALL = ("row", "col")
LANES = 128
BF16, F32 = jnp.bfloat16, jnp.float32
NT = (((1,), (1,)), ((), ()))


def room(mebibytes):
    return pltpu.CompilerParams(vmem_limit_bytes=mebibytes * 1024 * 1024)


def exchange(chunks):
    return lax.all_to_all(chunks, ALL, split_axis=0, concat_axis=0, tiled=True)


def cost(flops, bytes_accessed):
    return pl.CostEstimate(flops=flops, bytes_accessed=bytes_accessed, transcendentals=0)


def mixing_weights(lam, coef, angular_coef, nlam):
    coef_table = (coef[..., None] == jnp.arange(angular_coef.shape[0], dtype=coef.dtype)).astype(F32)
    coef_value = jnp.sum(coef_table * angular_coef, axis=-1)
    lam_table = (lam[..., None] == jnp.arange(nlam, dtype=lam.dtype)).astype(F32)
    return jnp.sum(coef_value[..., None] * lam_table, axis=-2)


def weights_to_radial(mixing, kernels):
    chans, strips, nlam = mixing.shape
    radial = jnp.dot(mixing.reshape(chans * strips, nlam), kernels, precision=lax.Precision.HIGHEST)
    return radial.reshape(chans, strips, kernels.shape[1])


def pick_kernel(
    own,
    pivots_at,
    lam_at,
    coef_at,
    count_at,
    rows,
    form_strip_at,
    out,
    pivots,
    lam,
    coef,
    count,
    form_strip,
    acc,
    pieces,
    chunks,
    small,
    sems,
    done,
):
    pairs = ((form_strip_at, form_strip), (pivots_at, pivots), (lam_at, lam), (coef_at, coef), (count_at, count))
    loads = [pltpu.make_async_copy(source, target, small.at[i]) for i, (source, target) in enumerate(pairs)]
    for load in loads:
        load.start()
    npiv = pivots.shape[1]
    local, nrad = rows.shape
    nstrip, chans = count.shape
    terms = lam.shape[0] // nstrip
    nmom = local // chans
    steps = sems.shape[0]
    depth = local // steps
    ndev, deep1, _ = out.shape
    copies = [
        pltpu.make_async_copy(rows.at[pl.ds(s * depth, depth), :], pieces.at[s], sems.at[s]) for s in range(steps)
    ]
    for copy in copies:
        copy.start()
    row = lax.axis_index("row")
    me = row * lax.axis_size("col") + lax.axis_index("col")
    for load in loads:
        load.wait()
    tall = deep1 - own * acc.shape[1] // LANES
    halves = nmom // tall
    half, part = lax.rem(row, halves), lax.div(row, halves)
    share = form_strip[
        0,
        pl.ds(pl.multiple_of(half * tall, tall), tall),
        pl.ds(pl.multiple_of(part * LANES, LANES), LANES),
    ]
    chunks[:, :tall, :] = jnp.broadcast_to(share[None], (ndev, tall, LANES))
    column = jnp.broadcast_to(pivots[...].astype(F32), (LANES, npiv)).T[:, :1].astype(jnp.int32) - me * local
    counts = jnp.broadcast_to(count[...][:, None, :], (nstrip, terms, chans)).reshape(nstrip * terms, chans)
    position = lax.rem(lax.broadcasted_iota(jnp.int32, (nstrip * terms, chans), 0), terms)
    order = jnp.where(position < counts, lam[...], LANES)
    table = jnp.concatenate([order, coef[...]], axis=0).astype(F32).astype(BF16)
    first = lax.broadcasted_iota(jnp.int32, (npiv, chans), 1) * nmom
    pick = jnp.logical_and(column >= first, column < first + nmom).astype(F32).astype(BF16)
    acc[:, nrad:] = lax.dot_general(pick, table, NT, preferred_element_type=F32)
    total = None
    for s in range(steps):
        pick = (column - s * depth == lax.broadcasted_iota(jnp.int32, (npiv, depth), 1)).astype(F32).astype(BF16)
        copies[s].wait()
        part = jnp.dot(pick, pieces[s], preferred_element_type=F32)
        total = part if total is None else total + part
    acc[:, :nrad] = total
    groups = done.shape[0]
    per = ndev // groups
    low = lax.broadcasted_iota(jnp.int32, (per // 2, 2 * own, LANES), 1) < own
    sends = []
    for g in range(groups):
        tiles = []
        for at in range(0, acc.shape[1], 2 * LANES):
            left = acc[g * per * own : (g + 1) * per * own, at : at + LANES].reshape(per // 2, 2 * own, LANES)
            right = acc[g * per * own : (g + 1) * per * own, at + LANES : at + 2 * LANES].reshape(
                per // 2, 2 * own, LANES
            )
            even = jnp.where(low, left, pltpu.roll(right, own, 1))
            odd = jnp.where(low, pltpu.roll(left, own, 1), right)
            tiles.append(jnp.stack([even, odd], axis=1).reshape(per, 2 * own, LANES))
        chunks[g * per : (g + 1) * per, tall:, :] = jnp.concatenate(tiles, axis=1).astype(BF16)
        send = pltpu.make_async_copy(chunks.at[pl.ds(g * per, per)], out.at[pl.ds(g * per, per)], done.at[g])
        send.start()
        sends.append(send)
    for send in sends:
        send.wait()


def strip_copies(got, strip, sems):
    nstrip, nmom, nrad = strip.shape
    nrow = got.shape[0] // nstrip
    halves = nrow * LANES // nrad
    tall = nmom // halves
    return [
        pltpu.make_async_copy(
            got.at[pl.ds(row * nstrip, nstrip), pl.ds(0, tall), :],
            strip.at[:, pl.ds(row % halves * tall, tall), pl.ds(row // halves * LANES, LANES)],
            sems.at[row],
        )
        for row in range(nrow)
    ]


def chosen_kernel(
    own, got, kernels_at, angular_at, kept, second, mail, kernels, angular, strip, wave, loads, sent
):
    del kept
    nstrip, nmom, nrad = strip.shape
    ndev, deep1, _ = got.shape
    nrow = ndev // nstrip
    parts = nrad // LANES
    halves = nrow // parts
    tall = nmom // halves
    first = [
        pltpu.make_async_copy(got.at[:, pl.ds(tall, deep1 - tall), :], mail, loads.at[nrow]),
        pltpu.make_async_copy(kernels_at, kernels, loads.at[nrow + 1]),
        pltpu.make_async_copy(angular_at, angular, loads.at[nrow + 2]),
    ]
    later = strip_copies(got, strip, loads)
    for copy in first + later:
        copy.start()
    for copy in first:
        copy.wait()
    mine = jnp.sum(mail[...].astype(F32), axis=0)
    nlam = kernels.shape[0]
    ncoef = angular.shape[0]
    terms = LANES // nstrip
    diagonal = (
        lax.broadcasted_iota(jnp.int32, (nstrip, LANES), 0)
        == lax.broadcasted_iota(jnp.int32, (nstrip, LANES), 1) // terms
    )
    coefs = lax.broadcasted_iota(jnp.int32, (ncoef, LANES), 0).astype(F32)
    lams = lax.broadcasted_iota(jnp.int32, (nlam, LANES), 0).astype(F32)
    lefts, rights, forms = [], [], []
    for a in range(own):
        lam = mine[parts * own + a : parts * own + a + 1, :]
        coef = mine[(parts + 1) * own + a : (parts + 1) * own + a + 1, :]
        value = jnp.sum(jnp.where(coef == coefs, angular[...], 0.0), axis=0, keepdims=True)
        left = jnp.where(diagonal, value, 0.0)
        lefts.append(
            jnp.concatenate([left if b == a else jnp.zeros_like(left) for b in range(own)], axis=1)
        )
        rights.append((lam == lams).astype(F32))
        form = jnp.concatenate([mine[g * own + a : g * own + a + 1, :] for g in range(parts)], axis=1)
        forms.append(jnp.broadcast_to(form, (nstrip, nrad)))
    mixing = lax.dot_general(
        jnp.concatenate(lefts, axis=0),
        jnp.concatenate(rights, axis=1),
        NT,
        precision=lax.Precision.HIGHEST,
        preferred_element_type=F32,
    )
    radial = jnp.dot(mixing, kernels[...], precision=lax.Precision.HIGHEST, preferred_element_type=F32)
    scaled = (jnp.concatenate(forms, axis=0) * radial).astype(BF16)
    scols = nstrip * nmom
    for copy in later:
        copy.wait()
    full = lax.dot_general(scaled, strip[...].reshape(scols, nrad), NT, preferred_element_type=F32)
    keep = (
        lax.broadcasted_iota(jnp.int32, (nstrip, scols), 0)
        == lax.broadcasted_iota(jnp.int32, (nstrip, scols), 1) // nmom
    )
    chosen = [
        jnp.sum(jnp.where(keep, full[a * nstrip : (a + 1) * nstrip], 0.0), axis=0, keepdims=True) for a in range(own)
    ]
    chosen = jnp.concatenate(chosen, axis=0)
    many, rows, wide = wave.shape
    tile = jnp.concatenate([chosen[:, at : at + wide] for at in range(0, scols, wide)], axis=0).astype(BF16)
    wave[...] = jnp.broadcast_to(tile[None], wave.shape)
    sends = []
    for g in range(ndev // many):
        send = pltpu.make_async_copy(
            wave, second.at[pl.ds(g * many, many), pl.ds(second.shape[1] - rows, rows), :], sent.at[g]
        )
        send.start()
        sends.append(send)
    for send in sends:
        send.wait()


def assemble_kernel(rows, radial, got, out, strip, sems):
    group, nrow, nmom, nrad = rows.shape
    nstrip = strip.shape[0]
    copies = strip_copies(got, strip, sems)
    for copy in copies:
        copy.start()
    for copy in copies:
        copy.wait()

    def one(p, carry):
        forms = [rows[q, p].astype(F32) for q in range(group)]
        for j in range(nstrip):
            scaled = jnp.concatenate(
                [(forms[q] * radial[q, p, j : j + 1, :]).astype(BF16) for q in range(group)], axis=0
            )
            block = lax.dot_general(strip[j], scaled, NT, preferred_element_type=F32)
            out[p, j * nmom : (j + 1) * nmom, :] = block.astype(BF16)
        return carry

    lax.fori_loop(0, nrow, one, 0)


def update_kernel(
    own, got, lower, blocks, out, upper_t, waves, low, columns, before, upper_all, spread, chosen, results, sems, sent
):
    npiv, scols = chosen.shape
    ndev, rows, wide = waves.shape
    nrow, ncol, deep, _ = columns.shape
    wave = pltpu.make_async_copy(got.at[:, pl.ds(deep, rows), :], waves, sems.at[2 * nrow])
    wave.start()
    bottom = pltpu.make_async_copy(lower, low, sems.at[2 * nrow + 1])
    bottom.start()
    loads = []
    for p in range(nrow):
        load = (
            pltpu.make_async_copy(got.at[pl.ds(p * ncol, ncol), pl.ds(0, deep), :], columns.at[p], sems.at[p]),
            pltpu.make_async_copy(blocks.at[p], before.at[p], sems.at[nrow + p]),
        )
        for copy in load:
            copy.start()
        loads.append(load)
    wave.wait()
    for b in range(wide // LANES):
        spread[b] = waves[:, :, b * LANES : (b + 1) * LANES].astype(F32).reshape(ndev * rows, LANES)
        for h in range(scols // wide):
            start = h * wide + b * LANES
            for a in range(own):
                chosen[a * ndev : (a + 1) * ndev, start : start + LANES] = spread[
                    b, pl.ds(h * own + a, ndev, stride=rows), :
                ].astype(BF16)
    bottom.wait()
    low1 = low[...].astype(BF16)
    low2 = (low[...] - low1.astype(F32)).astype(BF16)
    for at in range(0, scols, wide):
        rows_of = chosen[:, at : at + wide]
        upper = jnp.dot(low1, rows_of, preferred_element_type=F32) + jnp.dot(
            low2, rows_of, preferred_element_type=F32
        )
        upper_all[at : at + wide, :] = upper.T.astype(BF16)
    width = upper_t.shape[0]
    upper_t[...] = upper_all[pl.ds(pl.multiple_of(lax.axis_index("col") * width, width), width), :]
    for load in loads:
        for copy in load:
            copy.wait()
    sends = []
    for p in range(nrow):
        change = jnp.dot(upper_all[...], columns[p].reshape(npiv, wide), preferred_element_type=F32)
        results[p] = (before[p].astype(F32) - change).astype(BF16)
        send = pltpu.make_async_copy(results.at[p], out.at[p], sent.at[p])
        send.start()
        sends.append(send)
    for send in sends:
        send.wait()


def widen_kernel(got, out, broad, sent):
    ndev, width, wide = got.shape
    steps = sent.shape[0]
    many = ndev // steps
    sends = []
    for s in range(steps):
        for b in range(s * many, (s + 1) * many):
            broad[:, b * wide : (b + 1) * wide] = got[b].astype(F32)
        span = pl.ds(s * many * wide, many * wide)
        send = pltpu.make_async_copy(broad.at[:, span], out.at[:, span], sent.at[s])
        send.start()
        sends.append(send)
    for send in sends:
        send.wait()


def shards(
    form_rows,
    form_strip,
    lam_index,
    coef_index,
    term_count,
    angular_coef,
    kernels,
    pivots,
    lower_inverse,
    panel,
):
    nrow = lax.axis_size("row")
    ncol = lax.axis_size("col")
    ndev = nrow * ncol
    chans, nmom, nrad = form_rows.shape
    nstrip, terms = lam_index.shape[1:]
    nlam = kernels.shape[0]
    npiv = pivots.shape[0]
    scols = nstrip * nmom
    width = scols // ncol
    own = npiv // ndev
    group = chans // nrow
    local = chans * nmom
    vmem = pl.BlockSpec(memory_space=pltpu.VMEM)
    anywhere = pl.BlockSpec(memory_space=pl.ANY)
    dma = pltpu.SemaphoreType.DMA

    parts = nrad // LANES
    halves = nrow // parts
    tall = nmom // halves
    extra = 2 * nstrip * terms
    deep1 = tall + own * (nrad + extra) // LANES
    steps, groups = 4, 4
    first = pl.pallas_call(
        functools.partial(pick_kernel, own),
        out_shape=jax.ShapeDtypeStruct((ndev, deep1, LANES), BF16),
        in_specs=[anywhere] * 6,
        out_specs=anywhere,
        scratch_shapes=[
            pltpu.VMEM((1, npiv), jnp.int32),
            pltpu.VMEM((nstrip * terms, chans), jnp.int32),
            pltpu.VMEM((nstrip * terms, chans), jnp.int32),
            pltpu.VMEM((nstrip, chans), jnp.int32),
            pltpu.VMEM(form_strip.shape, BF16),
            pltpu.VMEM((npiv, nrad + extra), F32),
            pltpu.VMEM((steps, local // steps, nrad), BF16),
            pltpu.VMEM((ndev, deep1, LANES), BF16),
            dma((5,)),
            dma((steps,)),
            dma((groups,)),
        ],
        compiler_params=room(56),
        cost_estimate=cost(2 * npiv * local * nrad, 4 << 20),
        name="pick_pivots",
    )(
        pivots[None, :],
        lam_index.transpose(1, 2, 0).reshape(nstrip * terms, chans),
        coef_index.transpose(1, 2, 0).reshape(nstrip * terms, chans),
        term_count.T,
        form_rows.reshape(local, nrad),
        form_strip,
    )
    got = exchange(first)

    deep, wide = panel.shape[0], panel.shape[1] // ndev
    cut = panel.reshape(deep, ndev, wide).transpose(1, 0, 2)
    wave_rows = own * scols // wide
    second = jnp.pad(cut, ((0, 0), (0, wave_rows), (0, 0)))
    many = 32
    second = pl.pallas_call(
        functools.partial(chosen_kernel, own),
        out_shape=jax.ShapeDtypeStruct(second.shape, BF16),
        in_specs=[anywhere] * 4,
        out_specs=anywhere,
        scratch_shapes=[
            pltpu.VMEM((ndev, deep1 - tall, LANES), BF16),
            pltpu.VMEM(kernels.shape, F32),
            pltpu.VMEM((angular_coef.shape[0], 1), F32),
            pltpu.VMEM((nstrip, nmom, nrad), BF16),
            pltpu.VMEM((many, wave_rows, wide), BF16),
            dma((nrow + 3,)),
            dma((ndev // many,)),
        ],
        input_output_aliases={3: 0},
        compiler_params=room(61),
        cost_estimate=cost(2 * own * nstrip * scols * nrad, 4 << 20),
        name="chosen_rows",
    )(got, kernels, angular_coef[:, None], second)
    got2 = exchange(second)

    position = lax.broadcasted_iota(jnp.int32, lam_index.shape, 2)
    lam = jnp.where(position < term_count[:, :, None], lam_index, nlam)
    mixing = mixing_weights(lam, coef_index, angular_coef, nlam)
    radial = weights_to_radial(mixing, kernels)
    blocks = pl.pallas_call(
        assemble_kernel,
        out_shape=jax.ShapeDtypeStruct((nrow, scols, group * nmom), BF16),
        in_specs=[vmem, vmem, anywhere],
        out_specs=vmem,
        scratch_shapes=[pltpu.VMEM((nstrip, nmom, nrad), BF16), dma((nrow,))],
        compiler_params=room(56),
        cost_estimate=cost(2 * local * scols * nrad * 4, 8 << 20),
        name="assemble_strip",
    )(form_rows.reshape(group, nrow, nmom, nrad), radial.reshape(group, nrow, nstrip, nrad), got)

    lower = lower_inverse.reshape(npiv, ndev, own).transpose(0, 2, 1).reshape(npiv, npiv)
    done, upper_t = pl.pallas_call(
        functools.partial(update_kernel, own),
        out_shape=(
            jax.ShapeDtypeStruct((nrow, scols, wide), BF16),
            jax.ShapeDtypeStruct((width, npiv), BF16),
        ),
        in_specs=[anywhere, anywhere, anywhere],
        out_specs=(anywhere, vmem),
        scratch_shapes=[
            pltpu.VMEM((ndev, wave_rows, wide), BF16),
            pltpu.VMEM((npiv, npiv), F32),
            pltpu.VMEM((nrow, ncol, deep, wide), BF16),
            pltpu.VMEM((nrow, scols, wide), BF16),
            pltpu.VMEM((scols, npiv), BF16),
            pltpu.VMEM((wide // LANES, ndev * wave_rows, LANES), F32),
            pltpu.VMEM((npiv, scols), BF16),
            pltpu.VMEM((nrow, scols, wide), BF16),
            dma((2 * nrow + 2,)),
            dma((nrow,)),
        ],
        compiler_params=room(56),
        cost_estimate=cost(2 * npiv * scols * (3 * npiv + local), 12 << 20),
        name="update_blocks",
    )(got2, lower, blocks)
    final = exchange(done.reshape(ndev, width, wide))
    steps = 16
    trailing = pl.pallas_call(
        widen_kernel,
        out_shape=jax.ShapeDtypeStruct((width, ndev * wide), F32),
        in_specs=[vmem],
        out_specs=anywhere,
        scratch_shapes=[pltpu.VMEM((width, ndev * wide), F32), dma((steps,))],
        compiler_params=room(20),
        cost_estimate=cost(ndev * width * wide, 12 << 20),
        name="widen_blocks",
    )(final)
    return (trailing, upper_t)


def solution(mesh):
    in_specs = (
        P(("row", "col"), None, None),
        P("col", None, None),
        P(("row", "col"), None, None),
        P(("row", "col"), None, None),
        P(("row", "col"), None),
        P(),
        P(),
        P(),
        P(),
        P("col", "row"),
    )
    out_specs = (P("col", "row"), P("col", None))
    return jax.shard_map(shards, mesh=mesh, in_specs=in_specs, out_specs=out_specs, check_vma=False)
```

```python
import functools

import jax
import jax.numpy as jnp
from jax import lax
from jax.experimental import pallas as pl
from jax.experimental.pallas import tpu as pltpu
from jax.sharding import PartitionSpec as P

ALL = ("row", "col")
LANES = 128
BF16, F32 = jnp.bfloat16, jnp.float32
NT = (((1,), (1,)), ((), ()))


def room(mebibytes):
    return pltpu.CompilerParams(vmem_limit_bytes=mebibytes * 1024 * 1024)


def exchange(chunks):
    return lax.all_to_all(chunks, ALL, split_axis=0, concat_axis=0, tiled=True)


def cost(flops, bytes_accessed):
    return pl.CostEstimate(flops=flops, bytes_accessed=bytes_accessed, transcendentals=0)


def mixing_weights(lam, coef, angular_coef, nlam):
    coef_table = (coef[..., None] == jnp.arange(angular_coef.shape[0], dtype=coef.dtype)).astype(F32)
    coef_value = jnp.sum(coef_table * angular_coef, axis=-1)
    lam_table = (lam[..., None] == jnp.arange(nlam, dtype=lam.dtype)).astype(F32)
    return jnp.sum(coef_value[..., None] * lam_table, axis=-2)


def weights_to_radial(mixing, kernels):
    chans, strips, nlam = mixing.shape
    radial = jnp.dot(mixing.reshape(chans * strips, nlam), kernels, precision=lax.Precision.HIGHEST)
    return radial.reshape(chans, strips, kernels.shape[1])


def pick_kernel(
    own,
    pivots_at,
    lam_at,
    coef_at,
    count_at,
    rows,
    form_strip_at,
    out,
    pivots,
    lam,
    coef,
    count,
    form_strip,
    acc,
    pieces,
    chunks,
    small,
    sems,
    done,
):
    pairs = ((form_strip_at, form_strip), (pivots_at, pivots), (lam_at, lam), (coef_at, coef), (count_at, count))
    loads = [pltpu.make_async_copy(source, target, small.at[i]) for i, (source, target) in enumerate(pairs)]
    for load in loads:
        load.start()
    npiv = pivots.shape[1]
    local, nrad = rows.shape
    nstrip, chans = count.shape
    terms = lam.shape[0] // nstrip
    nmom = local // chans
    steps = sems.shape[0]
    depth = local // steps
    ndev, deep1, _ = out.shape
    copies = [
        pltpu.make_async_copy(rows.at[pl.ds(s * depth, depth), :], pieces.at[s], sems.at[s]) for s in range(steps)
    ]
    for copy in copies:
        copy.start()
    row = lax.axis_index("row")
    me = row * lax.axis_size("col") + lax.axis_index("col")
    for load in loads:
        load.wait()
    tall = deep1 - own * acc.shape[1] // LANES
    halves = nmom // tall
    half, part = lax.rem(row, halves), lax.div(row, halves)
    share = form_strip[
        0,
        pl.ds(pl.multiple_of(half * tall, tall), tall),
        pl.ds(pl.multiple_of(part * LANES, LANES), LANES),
    ]
    chunks[:, :tall, :] = jnp.broadcast_to(share[None], (ndev, tall, LANES))
    column = jnp.broadcast_to(pivots[...].astype(F32), (LANES, npiv)).T[:, :1].astype(jnp.int32) - me * local
    counts = jnp.broadcast_to(count[...][:, None, :], (nstrip, terms, chans)).reshape(nstrip * terms, chans)
    position = lax.rem(lax.broadcasted_iota(jnp.int32, (nstrip * terms, chans), 0), terms)
    order = jnp.where(position < counts, lam[...], LANES)
    table = jnp.concatenate([order, coef[...]], axis=0).astype(F32).astype(BF16)
    first = lax.broadcasted_iota(jnp.int32, (npiv, chans), 1) * nmom
    pick = jnp.logical_and(column >= first, column < first + nmom).astype(F32).astype(BF16)
    acc[:, nrad:] = lax.dot_general(pick, table, NT, preferred_element_type=F32)
    total = None
    for s in range(steps):
        pick = (column - s * depth == lax.broadcasted_iota(jnp.int32, (npiv, depth), 1)).astype(F32).astype(BF16)
        copies[s].wait()
        part = jnp.dot(pick, pieces[s], preferred_element_type=F32)
        total = part if total is None else total + part
    acc[:, :nrad] = total
    groups = done.shape[0]
    per = ndev // groups
    low = lax.broadcasted_iota(jnp.int32, (per // 2, 2 * own, LANES), 1) < own
    sends = []
    for g in range(groups):
        tiles = []
        for at in range(0, acc.shape[1], 2 * LANES):
            left = acc[g * per * own : (g + 1) * per * own, at : at + LANES].reshape(per // 2, 2 * own, LANES)
            right = acc[g * per * own : (g + 1) * per * own, at + LANES : at + 2 * LANES].reshape(
                per // 2, 2 * own, LANES
            )
            even = jnp.where(low, left, pltpu.roll(right, own, 1))
            odd = jnp.where(low, pltpu.roll(left, own, 1), right)
            tiles.append(jnp.stack([even, odd], axis=1).reshape(per, 2 * own, LANES))
        chunks[g * per : (g + 1) * per, tall:, :] = jnp.concatenate(tiles, axis=1).astype(BF16)
        send = pltpu.make_async_copy(chunks.at[pl.ds(g * per, per)], out.at[pl.ds(g * per, per)], done.at[g])
        send.start()
        sends.append(send)
    for send in sends:
        send.wait()


def strip_copies(got, strip, sems):
    nstrip, nmom, nrad = strip.shape
    nrow = got.shape[0] // nstrip
    halves = nrow * LANES // nrad
    tall = nmom // halves
    return [
        pltpu.make_async_copy(
            got.at[pl.ds(row * nstrip, nstrip), pl.ds(0, tall), :],
            strip.at[:, pl.ds(row % halves * tall, tall), pl.ds(row // halves * LANES, LANES)],
            sems.at[row],
        )
        for row in range(nrow)
    ]


def chosen_kernel(
    own, got, kernels_at, angular_at, kept, second, mail, kernels, angular, strip, wave, loads, sent
):
    del kept
    nstrip, nmom, nrad = strip.shape
    ndev, deep1, _ = got.shape
    nrow = ndev // nstrip
    parts = nrad // LANES
    halves = nrow // parts
    tall = nmom // halves
    first = [
        pltpu.make_async_copy(got.at[:, pl.ds(tall, deep1 - tall), :], mail, loads.at[nrow]),
        pltpu.make_async_copy(kernels_at, kernels, loads.at[nrow + 1]),
        pltpu.make_async_copy(angular_at, angular, loads.at[nrow + 2]),
    ]
    later = strip_copies(got, strip, loads)
    for copy in first + later:
        copy.start()
    for copy in first:
        copy.wait()
    mine = jnp.sum(mail[...].astype(F32), axis=0)
    nlam = kernels.shape[0]
    ncoef = angular.shape[0]
    terms = LANES // nstrip
    diagonal = (
        lax.broadcasted_iota(jnp.int32, (nstrip, LANES), 0)
        == lax.broadcasted_iota(jnp.int32, (nstrip, LANES), 1) // terms
    )
    coefs = lax.broadcasted_iota(jnp.int32, (ncoef, LANES), 0).astype(F32)
    lams = lax.broadcasted_iota(jnp.int32, (nlam, LANES), 0).astype(F32)
    lefts, rights, forms = [], [], []
    for a in range(own):
        lam = mine[parts * own + a : parts * own + a + 1, :]
        coef = mine[(parts + 1) * own + a : (parts + 1) * own + a + 1, :]
        value = jnp.sum(jnp.where(coef == coefs, angular[...], 0.0), axis=0, keepdims=True)
        left = jnp.where(diagonal, value, 0.0)
        lefts.append(
            jnp.concatenate([left if b == a else jnp.zeros_like(left) for b in range(own)], axis=1)
        )
        rights.append((lam == lams).astype(F32))
        form = jnp.concatenate([mine[g * own + a : g * own + a + 1, :] for g in range(parts)], axis=1)
        forms.append(jnp.broadcast_to(form, (nstrip, nrad)))
    mixing = lax.dot_general(
        jnp.concatenate(lefts, axis=0),
        jnp.concatenate(rights, axis=1),
        NT,
        precision=lax.Precision.HIGHEST,
        preferred_element_type=F32,
    )
    radial = jnp.dot(mixing, kernels[...], precision=lax.Precision.HIGHEST, preferred_element_type=F32)
    scaled = (jnp.concatenate(forms, axis=0) * radial).astype(BF16)
    scols = nstrip * nmom
    for copy in later:
        copy.wait()
    full = lax.dot_general(scaled, strip[...].reshape(scols, nrad), NT, preferred_element_type=F32)
    keep = (
        lax.broadcasted_iota(jnp.int32, (nstrip, scols), 0)
        == lax.broadcasted_iota(jnp.int32, (nstrip, scols), 1) // nmom
    )
    chosen = [
        jnp.sum(jnp.where(keep, full[a * nstrip : (a + 1) * nstrip], 0.0), axis=0, keepdims=True) for a in range(own)
    ]
    chosen = jnp.concatenate(chosen, axis=0)
    many, rows, wide = wave.shape
    tile = jnp.concatenate([chosen[:, at : at + wide] for at in range(0, scols, wide)], axis=0).astype(BF16)
    wave[...] = jnp.broadcast_to(tile[None], wave.shape)
    sends = []
    for g in range(ndev // many):
        send = pltpu.make_async_copy(
            wave, second.at[pl.ds(g * many, many), pl.ds(second.shape[1] - rows, rows), :], sent.at[g]
        )
        send.start()
        sends.append(send)
    for send in sends:
        send.wait()


def assemble_kernel(rows, radial, got, lower, out, strip, results, sems, sent):
    group, nrow, nmom, nrad = rows.shape
    nstrip = strip.shape[0]
    npiv = lower.shape[0]
    wide = results.shape[2]
    copies = strip_copies(got, strip, sems)
    for copy in copies:
        copy.start()
    low1 = lower[...].astype(BF16)
    low2 = (lower[...] - low1.astype(F32)).astype(BF16)
    for i, low in enumerate((low1, low2)):
        for at in range(0, npiv, wide):
            results[nrow + i, at // wide * npiv : (at // wide + 1) * npiv, :] = low[:, at : at + wide]
    for copy in copies:
        copy.wait()

    def send(p):
        return pltpu.make_async_copy(results.at[p], out.at[p], sent.at[p])

    def one(p, carry):
        forms = [rows[q, p].astype(F32) for q in range(group)]
        for j in range(nstrip):
            scaled = jnp.concatenate(
                [(forms[q] * radial[q, p, j : j + 1, :]).astype(BF16) for q in range(group)], axis=0
            )
            block = lax.dot_general(strip[j], scaled, NT, preferred_element_type=F32)
            results[p, j * nmom : (j + 1) * nmom, :] = block.astype(BF16)
        send(p).start()
        return carry

    send(nrow).start()
    send(nrow + 1).start()
    lax.fori_loop(0, nrow, one, 0)
    for p in range(nrow + 2):
        send(p).wait()


def update_kernel(own, got, blocks, out, upper_t, low1, low2, before, upper_all, spread, chosen, sems, low_sems):
    npiv, scols = chosen.shape
    ndev, deep2, wide = got.shape
    nrow = before.shape[0]
    ncol = ndev // nrow
    deep = npiv // ncol
    rows = deep2 - deep
    lows = []
    for i, low in enumerate((low1, low2)):
        for h in range(npiv // wide):
            lows.append(
                pltpu.make_async_copy(
                    blocks.at[nrow + i, pl.ds(h * npiv, npiv), :], low.at[:, pl.ds(h * wide, wide)], low_sems.at[i, h]
                )
            )
    loads = [pltpu.make_async_copy(blocks.at[p], before.at[p], sems.at[p]) for p in range(nrow)]
    for load in lows + loads:
        load.start()
    for b in range(wide // LANES):
        spread[b] = got[:, deep:, b * LANES : (b + 1) * LANES].astype(F32).reshape(ndev * rows, LANES)
        for h in range(scols // wide):
            start = h * wide + b * LANES
            for a in range(own):
                chosen[a * ndev : (a + 1) * ndev, start : start + LANES] = spread[
                    b, pl.ds(h * own + a, ndev, stride=rows), :
                ].astype(BF16)
    for load in lows:
        load.wait()
    for at in range(0, scols, wide):
        rows_of = chosen[:, at : at + wide]
        upper = jnp.dot(low1[...], rows_of, preferred_element_type=F32) + jnp.dot(
            low2[...], rows_of, preferred_element_type=F32
        )
        upper_all[at : at + wide, :] = upper.T.astype(BF16)
    width = upper_t.shape[0]
    upper_t[...] = upper_all[pl.ds(pl.multiple_of(lax.axis_index("col") * width, width), width), :]
    for load in loads:
        load.wait()
    for p in range(nrow):
        columns = got[p * ncol : (p + 1) * ncol, :deep, :].reshape(npiv, wide)
        change = jnp.dot(upper_all[...], columns, preferred_element_type=F32)
        out[p] = (before[p].astype(F32) - change).astype(BF16)


def widen_kernel(got, out, broad, sent):
    ndev, width, wide = got.shape
    steps = sent.shape[0]
    many = ndev // steps
    sends = []
    for s in range(steps):
        for b in range(s * many, (s + 1) * many):
            broad[:, b * wide : (b + 1) * wide] = got[b].astype(F32)
        span = pl.ds(s * many * wide, many * wide)
        send = pltpu.make_async_copy(broad.at[:, span], out.at[:, span], sent.at[s])
        send.start()
        sends.append(send)
    for send in sends:
        send.wait()


def shards(
    form_rows,
    form_strip,
    lam_index,
    coef_index,
    term_count,
    angular_coef,
    kernels,
    pivots,
    lower_inverse,
    panel,
):
    nrow = lax.axis_size("row")
    ncol = lax.axis_size("col")
    ndev = nrow * ncol
    chans, nmom, nrad = form_rows.shape
    nstrip, terms = lam_index.shape[1:]
    nlam = kernels.shape[0]
    npiv = pivots.shape[0]
    scols = nstrip * nmom
    width = scols // ncol
    own = npiv // ndev
    group = chans // nrow
    local = chans * nmom
    vmem = pl.BlockSpec(memory_space=pltpu.VMEM)
    anywhere = pl.BlockSpec(memory_space=pl.ANY)
    dma = pltpu.SemaphoreType.DMA

    parts = nrad // LANES
    halves = nrow // parts
    tall = nmom // halves
    extra = 2 * nstrip * terms
    deep1 = tall + own * (nrad + extra) // LANES
    steps, groups = 4, 4
    first = pl.pallas_call(
        functools.partial(pick_kernel, own),
        out_shape=jax.ShapeDtypeStruct((ndev, deep1, LANES), BF16),
        in_specs=[anywhere] * 6,
        out_specs=anywhere,
        scratch_shapes=[
            pltpu.VMEM((1, npiv), jnp.int32),
            pltpu.VMEM((nstrip * terms, chans), jnp.int32),
            pltpu.VMEM((nstrip * terms, chans), jnp.int32),
            pltpu.VMEM((nstrip, chans), jnp.int32),
            pltpu.VMEM(form_strip.shape, BF16),
            pltpu.VMEM((npiv, nrad + extra), F32),
            pltpu.VMEM((steps, local // steps, nrad), BF16),
            pltpu.VMEM((ndev, deep1, LANES), BF16),
            dma((5,)),
            dma((steps,)),
            dma((groups,)),
        ],
        compiler_params=room(56),
        cost_estimate=cost(2 * npiv * local * nrad, 4 << 20),
        name="pick_pivots",
    )(
        pivots[None, :],
        lam_index.transpose(1, 2, 0).reshape(nstrip * terms, chans),
        coef_index.transpose(1, 2, 0).reshape(nstrip * terms, chans),
        term_count.T,
        form_rows.reshape(local, nrad),
        form_strip,
    )
    got = exchange(first)

    deep, wide = panel.shape[0], panel.shape[1] // ndev
    cut = panel.reshape(deep, ndev, wide).transpose(1, 0, 2)
    wave_rows = own * scols // wide
    second = jnp.pad(cut, ((0, 0), (0, wave_rows), (0, 0)))
    many = 32
    second = pl.pallas_call(
        functools.partial(chosen_kernel, own),
        out_shape=jax.ShapeDtypeStruct(second.shape, BF16),
        in_specs=[anywhere] * 4,
        out_specs=anywhere,
        scratch_shapes=[
            pltpu.VMEM((ndev, deep1 - tall, LANES), BF16),
            pltpu.VMEM(kernels.shape, F32),
            pltpu.VMEM((angular_coef.shape[0], 1), F32),
            pltpu.VMEM((nstrip, nmom, nrad), BF16),
            pltpu.VMEM((many, wave_rows, wide), BF16),
            dma((nrow + 3,)),
            dma((ndev // many,)),
        ],
        input_output_aliases={3: 0},
        compiler_params=room(40),
        cost_estimate=cost(2 * own * nstrip * scols * nrad, 4 << 20),
        name="chosen_rows",
    )(got, kernels, angular_coef[:, None], second)
    got2 = exchange(second)

    position = lax.broadcasted_iota(jnp.int32, lam_index.shape, 2)
    lam = jnp.where(position < term_count[:, :, None], lam_index, nlam)
    mixing = mixing_weights(lam, coef_index, angular_coef, nlam)
    radial = weights_to_radial(mixing, kernels)
    lower = lower_inverse.reshape(npiv, ndev, own).transpose(0, 2, 1).reshape(npiv, npiv)
    slots = 10 * nrow
    blocks = pl.pallas_call(
        assemble_kernel,
        out_shape=jax.ShapeDtypeStruct((slots, scols, group * nmom), BF16),
        in_specs=[vmem, vmem, anywhere, vmem],
        out_specs=anywhere,
        scratch_shapes=[
            pltpu.VMEM((nstrip, nmom, nrad), BF16),
            pltpu.VMEM((nrow + 2, scols, group * nmom), BF16),
            dma((nrow,)),
            dma((nrow + 2,)),
        ],
        compiler_params=room(56),
        cost_estimate=cost(2 * local * scols * nrad * 4, 8 << 20),
        name="assemble_strip",
    )(form_rows.reshape(group, nrow, nmom, nrad), radial.reshape(group, nrow, nstrip, nrad), got, lower)

    done, upper_t = pl.pallas_call(
        functools.partial(update_kernel, own),
        out_shape=(
            jax.ShapeDtypeStruct((nrow, scols, wide), BF16),
            jax.ShapeDtypeStruct((width, npiv), BF16),
        ),
        in_specs=[vmem, anywhere],
        out_specs=(vmem, vmem),
        scratch_shapes=[
            pltpu.VMEM((npiv, npiv), BF16),
            pltpu.VMEM((npiv, npiv), BF16),
            pltpu.VMEM((nrow, scols, wide), BF16),
            pltpu.VMEM((scols, npiv), BF16),
            pltpu.VMEM((wide // LANES, ndev * wave_rows, LANES), F32),
            pltpu.VMEM((npiv, scols), BF16),
            dma((nrow,)),
            dma((2, npiv // wide)),
        ],
        compiler_params=room(24),
        cost_estimate=cost(2 * npiv * scols * (3 * npiv + local), 12 << 20),
        name="update_blocks",
    )(got2, blocks)
    final = exchange(done.reshape(ndev, width, wide))
    steps = 16
    trailing = pl.pallas_call(
        widen_kernel,
        out_shape=jax.ShapeDtypeStruct((width, ndev * wide), F32),
        in_specs=[vmem],
        out_specs=anywhere,
        scratch_shapes=[pltpu.VMEM((width, ndev * wide), F32), dma((steps,))],
        compiler_params=room(20),
        cost_estimate=cost(ndev * width * wide, 12 << 20),
        name="widen_blocks",
    )(final)
    return (trailing, upper_t)


def solution(mesh):
    in_specs = (
        P(("row", "col"), None, None),
        P("col", None, None),
        P(("row", "col"), None, None),
        P(("row", "col"), None, None),
        P(("row", "col"), None),
        P(),
        P(),
        P(),
        P(),
        P("col", "row"),
    )
    out_specs = (P("col", "row"), P("col", None))
    return jax.shard_map(shards, mesh=mesh, in_specs=in_specs, out_specs=out_specs, check_vma=False)
```

```python
import functools

import jax
import jax.numpy as jnp
from jax import lax
from jax.experimental import pallas as pl
from jax.experimental.pallas import tpu as pltpu
from jax.sharding import PartitionSpec as P

ALL = ("row", "col")
LANES = 128
CORES = 2
BF16, F32 = jnp.bfloat16, jnp.float32
NT = (((1,), (1,)), ((), ()))


def room(mebibytes):
    return pltpu.CompilerParams(vmem_limit_bytes=mebibytes * 1024 * 1024)


def exchange(chunks):
    return lax.all_to_all(chunks, ALL, split_axis=0, concat_axis=0, tiled=True)


def cost(flops, bytes_accessed):
    return pl.CostEstimate(flops=flops, bytes_accessed=bytes_accessed, transcendentals=0)


def mixing_weights(lam, coef, angular_coef, nlam):
    coef_table = (coef[..., None] == jnp.arange(angular_coef.shape[0], dtype=coef.dtype)).astype(F32)
    coef_value = jnp.sum(coef_table * angular_coef, axis=-1)
    lam_table = (lam[..., None] == jnp.arange(nlam, dtype=lam.dtype)).astype(F32)
    return jnp.sum(coef_value[..., None] * lam_table, axis=-2)


def weights_to_radial(mixing, kernels):
    chans, strips, nlam = mixing.shape
    radial = jnp.dot(mixing.reshape(chans * strips, nlam), kernels, precision=lax.Precision.HIGHEST)
    return radial.reshape(chans, strips, kernels.shape[1])


def pick_kernel(
    own,
    pivots_at,
    lam_at,
    coef_at,
    count_at,
    rows,
    form_strip_at,
    out,
    pivots,
    lam,
    coef,
    count,
    form_strip,
    acc,
    pieces,
    chunks,
    small,
    sems,
    done,
):
    pairs = ((form_strip_at, form_strip), (pivots_at, pivots), (lam_at, lam), (coef_at, coef), (count_at, count))
    loads = [pltpu.make_async_copy(source, target, small.at[i]) for i, (source, target) in enumerate(pairs)]
    for load in loads:
        load.start()
    npiv = pivots.shape[1]
    local, nrad = rows.shape
    nstrip, chans = count.shape
    terms = lam.shape[0] // nstrip
    nmom = local // chans
    steps = sems.shape[0]
    depth = local // steps
    ndev, deep1, _ = out.shape
    copies = [
        pltpu.make_async_copy(rows.at[pl.ds(s * depth, depth), :], pieces.at[s], sems.at[s]) for s in range(steps)
    ]
    for copy in copies:
        copy.start()
    row = lax.axis_index("row")
    me = row * lax.axis_size("col") + lax.axis_index("col")
    for load in loads:
        load.wait()
    tall = deep1 - own * acc.shape[1] // LANES
    ncol = lax.axis_size("col")
    half, part = lax.rem(row, CORES), lax.div(row, CORES)
    for core in range(CORES):
        start = half * CORES * tall + core * tall
        share = form_strip[
            0,
            pl.ds(pl.multiple_of(start, tall), tall),
            pl.ds(pl.multiple_of(part * LANES, LANES), LANES),
        ]
        for at in range(core * ncol, ndev, CORES * ncol):
            chunks[at : at + ncol, :tall, :] = jnp.broadcast_to(share[None], (ncol, tall, LANES))
    column = jnp.broadcast_to(pivots[...].astype(F32), (LANES, npiv)).T[:, :1].astype(jnp.int32) - me * local
    counts = jnp.broadcast_to(count[...][:, None, :], (nstrip, terms, chans)).reshape(nstrip * terms, chans)
    position = lax.rem(lax.broadcasted_iota(jnp.int32, (nstrip * terms, chans), 0), terms)
    order = jnp.where(position < counts, lam[...], LANES)
    table = jnp.concatenate([order, coef[...]], axis=0).astype(F32).astype(BF16)
    first = lax.broadcasted_iota(jnp.int32, (npiv, chans), 1) * nmom
    pick = jnp.logical_and(column >= first, column < first + nmom).astype(F32).astype(BF16)
    acc[:, nrad:] = lax.dot_general(pick, table, NT, preferred_element_type=F32)
    total = None
    for s in range(steps):
        pick = (column - s * depth == lax.broadcasted_iota(jnp.int32, (npiv, depth), 1)).astype(F32).astype(BF16)
        copies[s].wait()
        part = jnp.dot(pick, pieces[s], preferred_element_type=F32)
        total = part if total is None else total + part
    acc[:, :nrad] = total
    groups = done.shape[0]
    per = ndev // groups
    low = lax.broadcasted_iota(jnp.int32, (per // 2, 2 * own, LANES), 1) < own
    sends = []
    for g in range(groups):
        tiles = []
        for at in range(0, acc.shape[1], 2 * LANES):
            left = acc[g * per * own : (g + 1) * per * own, at : at + LANES].reshape(per // 2, 2 * own, LANES)
            right = acc[g * per * own : (g + 1) * per * own, at + LANES : at + 2 * LANES].reshape(
                per // 2, 2 * own, LANES
            )
            even = jnp.where(low, left, pltpu.roll(right, own, 1))
            odd = jnp.where(low, pltpu.roll(left, own, 1), right)
            tiles.append(jnp.stack([even, odd], axis=1).reshape(per, 2 * own, LANES))
        chunks[g * per : (g + 1) * per, tall:, :] = jnp.concatenate(tiles, axis=1).astype(BF16)
        send = pltpu.make_async_copy(chunks.at[pl.ds(g * per, per)], out.at[pl.ds(g * per, per)], done.at[g])
        send.start()
        sends.append(send)
    for send in sends:
        send.wait()


def strip_copies(got, other, strip, sems):
    nstrip, nmom, nrad = strip.shape
    nrow = got.shape[0] // nstrip
    tall = nmom // (CORES * CORES)
    core = lax.rem(lax.axis_index("row"), CORES)
    copies = []
    for i, (source, side) in enumerate(((got, core), (other, 1 - core))):
        for row in range(nrow):
            start = pl.multiple_of(row % CORES * CORES * tall + side * tall, tall)
            copies.append(
                pltpu.make_async_copy(
                    source.at[pl.ds(row * nstrip, nstrip), pl.ds(0, tall), :],
                    strip.at[:, pl.ds(start, tall), pl.ds(row // CORES * LANES, LANES)],
                    sems.at[i * nrow + row],
                )
            )
    return copies


def scale_kernel(own, nstrip, got, kernels_at, angular_at, scaled, mail, kernels, angular, loads):
    ndev, deep1, _ = got.shape
    nrad = kernels.shape[1]
    parts = nrad // LANES
    rows = mail.shape[1]
    first = [
        pltpu.make_async_copy(got.at[:, pl.ds(deep1 - rows, rows), :], mail, loads.at[0]),
        pltpu.make_async_copy(kernels_at, kernels, loads.at[1]),
        pltpu.make_async_copy(angular_at, angular, loads.at[2]),
    ]
    for copy in first:
        copy.start()
    for copy in first:
        copy.wait()
    mine = jnp.sum(mail[...].astype(F32), axis=0)
    nlam = kernels.shape[0]
    ncoef = angular.shape[0]
    terms = LANES // nstrip
    diagonal = (
        lax.broadcasted_iota(jnp.int32, (nstrip, LANES), 0)
        == lax.broadcasted_iota(jnp.int32, (nstrip, LANES), 1) // terms
    )
    coefs = lax.broadcasted_iota(jnp.int32, (ncoef, LANES), 0).astype(F32)
    lams = lax.broadcasted_iota(jnp.int32, (nlam, LANES), 0).astype(F32)
    lefts, rights, forms = [], [], []
    for a in range(own):
        lam = mine[parts * own + a : parts * own + a + 1, :]
        coef = mine[(parts + 1) * own + a : (parts + 1) * own + a + 1, :]
        value = jnp.sum(jnp.where(coef == coefs, angular[...], 0.0), axis=0, keepdims=True)
        left = jnp.where(diagonal, value, 0.0)
        lefts.append(
            jnp.concatenate([left if b == a else jnp.zeros_like(left) for b in range(own)], axis=1)
        )
        rights.append((lam == lams).astype(F32))
        form = jnp.concatenate([mine[g * own + a : g * own + a + 1, :] for g in range(parts)], axis=1)
        forms.append(jnp.broadcast_to(form, (nstrip, nrad)))
    mixing = lax.dot_general(
        jnp.concatenate(lefts, axis=0),
        jnp.concatenate(rights, axis=1),
        NT,
        precision=lax.Precision.HIGHEST,
        preferred_element_type=F32,
    )
    radial = jnp.dot(mixing, kernels[...], precision=lax.Precision.HIGHEST, preferred_element_type=F32)
    scaled[...] = (jnp.concatenate(forms, axis=0) * radial).astype(BF16)


def chosen_kernel(own, got, other, scaled, kept, second, strip, wave, loads, sent):
    del kept
    nstrip, nmom, nrad = strip.shape
    ndev = got.shape[0]
    copies = strip_copies(got, other, strip, loads)
    for copy in copies:
        copy.start()
    for copy in copies:
        copy.wait()
    scols = nstrip * nmom
    full = lax.dot_general(scaled[...], strip[...].reshape(scols, nrad), NT, preferred_element_type=F32)
    keep = (
        lax.broadcasted_iota(jnp.int32, (nstrip, scols), 0)
        == lax.broadcasted_iota(jnp.int32, (nstrip, scols), 1) // nmom
    )
    chosen = [
        jnp.sum(jnp.where(keep, full[a * nstrip : (a + 1) * nstrip], 0.0), axis=0, keepdims=True) for a in range(own)
    ]
    chosen = jnp.concatenate(chosen, axis=0)
    many, rows, wide = wave.shape
    tile = jnp.concatenate([chosen[:, at : at + wide] for at in range(0, scols, wide)], axis=0).astype(BF16)
    wave[...] = jnp.broadcast_to(tile[None], wave.shape)
    sends = []
    for g in range(ndev // many):
        send = pltpu.make_async_copy(
            wave, second.at[pl.ds(g * many, many), pl.ds(second.shape[1] - rows, rows), :], sent.at[g]
        )
        send.start()
        sends.append(send)
    for send in sends:
        send.wait()


def assemble_kernel(rows, radial, got, other, lower, out, strip, results, sems, sent):
    group, nrow, nmom, nrad = rows.shape
    nstrip = strip.shape[0]
    npiv = lower.shape[0]
    wide = results.shape[2]
    copies = strip_copies(got, other, strip, sems)
    for copy in copies:
        copy.start()
    low1 = lower[...].astype(BF16)
    low2 = (lower[...] - low1.astype(F32)).astype(BF16)
    for i, low in enumerate((low1, low2)):
        for at in range(0, npiv, wide):
            results[nrow + i, at // wide * npiv : (at // wide + 1) * npiv, :] = low[:, at : at + wide]
    for copy in copies:
        copy.wait()

    def send(p):
        return pltpu.make_async_copy(results.at[p], out.at[p], sent.at[p])

    def one(p, carry):
        forms = [rows[q, p].astype(F32) for q in range(group)]
        for j in range(nstrip):
            scaled = jnp.concatenate(
                [(forms[q] * radial[q, p, j : j + 1, :]).astype(BF16) for q in range(group)], axis=0
            )
            block = lax.dot_general(strip[j], scaled, NT, preferred_element_type=F32)
            results[p, j * nmom : (j + 1) * nmom, :] = block.astype(BF16)
        send(p).start()
        return carry

    send(nrow).start()
    send(nrow + 1).start()
    lax.fori_loop(0, nrow, one, 0)
    for p in range(nrow + 2):
        send(p).wait()


def update_kernel(own, got, blocks, out, upper_t, low1, low2, before, upper_all, spread, chosen, sems, low_sems):
    npiv, scols = chosen.shape
    ndev, deep2, wide = got.shape
    nrow = before.shape[0]
    ncol = ndev // nrow
    deep = npiv // ncol
    rows = deep2 - deep
    lows = []
    for i, low in enumerate((low1, low2)):
        for h in range(npiv // wide):
            lows.append(
                pltpu.make_async_copy(
                    blocks.at[nrow + i, pl.ds(h * npiv, npiv), :], low.at[:, pl.ds(h * wide, wide)], low_sems.at[i, h]
                )
            )
    loads = [pltpu.make_async_copy(blocks.at[p], before.at[p], sems.at[p]) for p in range(nrow)]
    for load in lows + loads:
        load.start()
    for b in range(wide // LANES):
        spread[b] = got[:, deep:, b * LANES : (b + 1) * LANES].astype(F32).reshape(ndev * rows, LANES)
        for h in range(scols // wide):
            start = h * wide + b * LANES
            for a in range(own):
                chosen[a * ndev : (a + 1) * ndev, start : start + LANES] = spread[
                    b, pl.ds(h * own + a, ndev, stride=rows), :
                ].astype(BF16)
    for load in lows:
        load.wait()
    for at in range(0, scols, wide):
        rows_of = chosen[:, at : at + wide]
        upper = jnp.dot(low1[...], rows_of, preferred_element_type=F32) + jnp.dot(
            low2[...], rows_of, preferred_element_type=F32
        )
        upper_all[at : at + wide, :] = upper.T.astype(BF16)
    width = upper_t.shape[0]
    upper_t[...] = upper_all[pl.ds(pl.multiple_of(lax.axis_index("col") * width, width), width), :]
    for load in loads:
        load.wait()
    for p in range(nrow):
        columns = got[p * ncol : (p + 1) * ncol, :deep, :].reshape(npiv, wide)
        change = jnp.dot(upper_all[...], columns, preferred_element_type=F32)
        out[p] = (before[p].astype(F32) - change).astype(BF16)


def widen_kernel(got, out, broad, sent):
    ndev, width, wide = got.shape
    steps = sent.shape[0]
    many = ndev // steps
    sends = []
    for s in range(steps):
        for b in range(s * many, (s + 1) * many):
            broad[:, b * wide : (b + 1) * wide] = got[b].astype(F32)
        span = pl.ds(s * many * wide, many * wide)
        send = pltpu.make_async_copy(broad.at[:, span], out.at[:, span], sent.at[s])
        send.start()
        sends.append(send)
    for send in sends:
        send.wait()


def shards(
    form_rows,
    form_strip,
    lam_index,
    coef_index,
    term_count,
    angular_coef,
    kernels,
    pivots,
    lower_inverse,
    panel,
):
    nrow = lax.axis_size("row")
    ncol = lax.axis_size("col")
    ndev = nrow * ncol
    chans, nmom, nrad = form_rows.shape
    nstrip, terms = lam_index.shape[1:]
    nlam = kernels.shape[0]
    npiv = pivots.shape[0]
    scols = nstrip * nmom
    width = scols // ncol
    own = npiv // ndev
    group = chans // nrow
    local = chans * nmom
    vmem = pl.BlockSpec(memory_space=pltpu.VMEM)
    anywhere = pl.BlockSpec(memory_space=pl.ANY)
    dma = pltpu.SemaphoreType.DMA

    tall = nmom // (CORES * CORES)
    extra = 2 * nstrip * terms
    deep1 = tall + own * (nrad + extra) // LANES
    steps, groups = 4, 4
    first = pl.pallas_call(
        functools.partial(pick_kernel, own),
        out_shape=jax.ShapeDtypeStruct((ndev, deep1, LANES), BF16),
        in_specs=[anywhere] * 6,
        out_specs=anywhere,
        scratch_shapes=[
            pltpu.VMEM((1, npiv), jnp.int32),
            pltpu.VMEM((nstrip * terms, chans), jnp.int32),
            pltpu.VMEM((nstrip * terms, chans), jnp.int32),
            pltpu.VMEM((nstrip, chans), jnp.int32),
            pltpu.VMEM(form_strip.shape, BF16),
            pltpu.VMEM((npiv, nrad + extra), F32),
            pltpu.VMEM((steps, local // steps, nrad), BF16),
            pltpu.VMEM((ndev, deep1, LANES), BF16),
            dma((5,)),
            dma((steps,)),
            dma((groups,)),
        ],
        compiler_params=room(56),
        cost_estimate=cost(2 * npiv * local * nrad, 4 << 20),
        name="pick_pivots",
    )(
        pivots[None, :],
        lam_index.transpose(1, 2, 0).reshape(nstrip * terms, chans),
        coef_index.transpose(1, 2, 0).reshape(nstrip * terms, chans),
        term_count.T,
        form_rows.reshape(local, nrad),
        form_strip,
    )
    deep, wide = panel.shape[0], panel.shape[1] // ndev
    cut = panel.reshape(deep, ndev, wide).transpose(1, 0, 2)
    wave_rows = own * scols // wide
    second = jnp.pad(cut, ((0, 0), (0, wave_rows), (0, 0)))
    got = exchange(first)
    got, second = lax.optimization_barrier((got, second))
    other = lax.ppermute(got, "row", [(i, i ^ 1) for i in range(nrow)])

    many = 32
    scaled = pl.pallas_call(
        functools.partial(scale_kernel, own, nstrip),
        out_shape=jax.ShapeDtypeStruct((own * nstrip, nrad), BF16),
        in_specs=[anywhere] * 3,
        out_specs=vmem,
        scratch_shapes=[
            pltpu.VMEM((ndev, deep1 - tall, LANES), BF16),
            pltpu.VMEM(kernels.shape, F32),
            pltpu.VMEM((angular_coef.shape[0], 1), F32),
            dma((3,)),
        ],
        compiler_params=room(40),
        cost_estimate=cost(2 * own * nstrip * nrad * LANES, 1 << 20),
        name="scale_pivots",
    )(got, kernels, angular_coef[:, None])
    second = pl.pallas_call(
        functools.partial(chosen_kernel, own),
        out_shape=jax.ShapeDtypeStruct(second.shape, BF16),
        in_specs=[anywhere, anywhere, vmem, anywhere],
        out_specs=anywhere,
        scratch_shapes=[
            pltpu.VMEM((nstrip, nmom, nrad), BF16),
            pltpu.VMEM((many, wave_rows, wide), BF16),
            dma((CORES * nrow,)),
            dma((ndev // many,)),
        ],
        input_output_aliases={3: 0},
        compiler_params=room(40),
        cost_estimate=cost(2 * own * nstrip * scols * nrad, 4 << 20),
        name="chosen_rows",
    )(got, other, scaled, second)
    got2 = exchange(second)

    position = lax.broadcasted_iota(jnp.int32, lam_index.shape, 2)
    lam = jnp.where(position < term_count[:, :, None], lam_index, nlam)
    mixing = mixing_weights(lam, coef_index, angular_coef, nlam)
    radial = weights_to_radial(mixing, kernels)
    lower = lower_inverse.reshape(npiv, ndev, own).transpose(0, 2, 1).reshape(npiv, npiv)
    slots = 10 * nrow
    blocks = pl.pallas_call(
        assemble_kernel,
        out_shape=jax.ShapeDtypeStruct((slots, scols, group * nmom), BF16),
        in_specs=[vmem, vmem, anywhere, anywhere, vmem],
        out_specs=anywhere,
        scratch_shapes=[
            pltpu.VMEM((nstrip, nmom, nrad), BF16),
            pltpu.VMEM((nrow + 2, scols, group * nmom), BF16),
            dma((CORES * nrow,)),
            dma((nrow + 2,)),
        ],
        compiler_params=room(56),
        cost_estimate=cost(2 * local * scols * nrad * 4, 8 << 20),
        name="assemble_strip",
    )(form_rows.reshape(group, nrow, nmom, nrad), radial.reshape(group, nrow, nstrip, nrad), got, other, lower)

    done, upper_t = pl.pallas_call(
        functools.partial(update_kernel, own),
        out_shape=(
            jax.ShapeDtypeStruct((nrow, scols, wide), BF16),
            jax.ShapeDtypeStruct((width, npiv), BF16),
        ),
        in_specs=[vmem, anywhere],
        out_specs=(vmem, vmem),
        scratch_shapes=[
            pltpu.VMEM((npiv, npiv), BF16),
            pltpu.VMEM((npiv, npiv), BF16),
            pltpu.VMEM((nrow, scols, wide), BF16),
            pltpu.VMEM((scols, npiv), BF16),
            pltpu.VMEM((wide // LANES, ndev * wave_rows, LANES), F32),
            pltpu.VMEM((npiv, scols), BF16),
            dma((nrow,)),
            dma((2, npiv // wide)),
        ],
        compiler_params=room(24),
        cost_estimate=cost(2 * npiv * scols * (3 * npiv + local), 12 << 20),
        name="update_blocks",
    )(got2, blocks)
    final = exchange(done.reshape(ndev, width, wide))
    steps = 16
    trailing = pl.pallas_call(
        widen_kernel,
        out_shape=jax.ShapeDtypeStruct((width, ndev * wide), F32),
        in_specs=[vmem],
        out_specs=anywhere,
        scratch_shapes=[pltpu.VMEM((width, ndev * wide), F32), dma((steps,))],
        compiler_params=room(20),
        cost_estimate=cost(ndev * width * wide, 12 << 20),
        name="widen_blocks",
    )(final)
    return (trailing, upper_t)


def solution(mesh):
    in_specs = (
        P(("row", "col"), None, None),
        P("col", None, None),
        P(("row", "col"), None, None),
        P(("row", "col"), None, None),
        P(("row", "col"), None),
        P(),
        P(),
        P(),
        P(),
        P("col", "row"),
    )
    out_specs = (P("col", "row"), P("col", None))
    return jax.shard_map(shards, mesh=mesh, in_specs=in_specs, out_specs=out_specs, check_vma=False)
```

```python
import functools

import jax
import jax.numpy as jnp
from jax import lax
from jax.experimental import pallas as pl
from jax.experimental.pallas import tpu as pltpu
from jax.sharding import PartitionSpec as P

ALL = ("row", "col")
LANES = 128
CORES = 2
BF16, F32 = jnp.bfloat16, jnp.float32
NT = (((1,), (1,)), ((), ()))


def room(mebibytes):
    return pltpu.CompilerParams(vmem_limit_bytes=mebibytes * 1024 * 1024)


def exchange(chunks):
    return lax.all_to_all(chunks, ALL, split_axis=0, concat_axis=0, tiled=True)


def cost(flops, bytes_accessed):
    return pl.CostEstimate(flops=flops, bytes_accessed=bytes_accessed, transcendentals=0)


def mixing_weights(lam, coef, angular_coef, nlam):
    coef_table = (coef[..., None] == jnp.arange(angular_coef.shape[0], dtype=coef.dtype)).astype(F32)
    coef_value = jnp.sum(coef_table * angular_coef, axis=-1)
    lam_table = (lam[..., None] == jnp.arange(nlam, dtype=lam.dtype)).astype(F32)
    return jnp.sum(coef_value[..., None] * lam_table, axis=-2)


def weights_to_radial(mixing, kernels):
    chans, strips, nlam = mixing.shape
    radial = jnp.dot(mixing.reshape(chans * strips, nlam), kernels, precision=lax.Precision.HIGHEST)
    return radial.reshape(chans, strips, kernels.shape[1])


def pick_kernel(
    own,
    pivots_at,
    lam_at,
    coef_at,
    count_at,
    rows,
    form_strip_at,
    out,
    pivots,
    lam,
    coef,
    count,
    form_strip,
    acc,
    pieces,
    chunks,
    small,
    sems,
    done,
):
    pairs = ((form_strip_at, form_strip), (pivots_at, pivots), (lam_at, lam), (coef_at, coef), (count_at, count))
    loads = [pltpu.make_async_copy(source, target, small.at[i]) for i, (source, target) in enumerate(pairs)]
    for load in loads:
        load.start()
    npiv = pivots.shape[1]
    local, nrad = rows.shape
    nstrip, chans = count.shape
    terms = lam.shape[0] // nstrip
    nmom = local // chans
    steps = sems.shape[0]
    depth = local // steps
    ndev, deep1, _ = out.shape
    copies = [
        pltpu.make_async_copy(rows.at[pl.ds(s * depth, depth), :], pieces.at[s], sems.at[s]) for s in range(steps)
    ]
    for copy in copies:
        copy.start()
    row = lax.axis_index("row")
    me = row * lax.axis_size("col") + lax.axis_index("col")
    for load in loads:
        load.wait()
    tall = deep1 - own * acc.shape[1] // LANES
    ncol = lax.axis_size("col")
    half, part = lax.rem(row, CORES), lax.div(row, CORES)
    for core in range(CORES):
        start = half * CORES * tall + core * tall
        share = form_strip[
            0,
            pl.ds(pl.multiple_of(start, tall), tall),
            pl.ds(pl.multiple_of(part * LANES, LANES), LANES),
        ]
        for at in range(core * ncol, ndev, CORES * ncol):
            chunks[at : at + ncol, :tall, :] = jnp.broadcast_to(share[None], (ncol, tall, LANES))
    column = jnp.broadcast_to(pivots[...].astype(F32), (LANES, npiv)).T[:, :1].astype(jnp.int32) - me * local
    counts = jnp.broadcast_to(count[...][:, None, :], (nstrip, terms, chans)).reshape(nstrip * terms, chans)
    position = lax.rem(lax.broadcasted_iota(jnp.int32, (nstrip * terms, chans), 0), terms)
    order = jnp.where(position < counts, lam[...], LANES)
    table = jnp.concatenate([order, coef[...]], axis=0).astype(F32).astype(BF16)
    first = lax.broadcasted_iota(jnp.int32, (npiv, chans), 1) * nmom
    pick = jnp.logical_and(column >= first, column < first + nmom).astype(F32).astype(BF16)
    acc[:, nrad:] = lax.dot_general(pick, table, NT, preferred_element_type=F32)
    total = None
    for s in range(steps):
        pick = (column - s * depth == lax.broadcasted_iota(jnp.int32, (npiv, depth), 1)).astype(F32).astype(BF16)
        copies[s].wait()
        part = jnp.dot(pick, pieces[s], preferred_element_type=F32)
        total = part if total is None else total + part
    acc[:, :nrad] = total
    groups = done.shape[0]
    per = ndev // groups
    low = lax.broadcasted_iota(jnp.int32, (per // 2, 2 * own, LANES), 1) < own
    sends = []
    for g in range(groups):
        tiles = []
        for at in range(0, acc.shape[1], 2 * LANES):
            left = acc[g * per * own : (g + 1) * per * own, at : at + LANES].reshape(per // 2, 2 * own, LANES)
            right = acc[g * per * own : (g + 1) * per * own, at + LANES : at + 2 * LANES].reshape(
                per // 2, 2 * own, LANES
            )
            even = jnp.where(low, left, pltpu.roll(right, own, 1))
            odd = jnp.where(low, pltpu.roll(left, own, 1), right)
            tiles.append(jnp.stack([even, odd], axis=1).reshape(per, 2 * own, LANES))
        chunks[g * per : (g + 1) * per, tall:, :] = jnp.concatenate(tiles, axis=1).astype(BF16)
        send = pltpu.make_async_copy(chunks.at[pl.ds(g * per, per)], out.at[pl.ds(g * per, per)], done.at[g])
        send.start()
        sends.append(send)
    for send in sends:
        send.wait()


def strip_copies(got, other, strip, sems):
    nstrip, nmom, nrad = strip.shape
    nrow = got.shape[0] // nstrip
    tall = nmom // (CORES * CORES)
    core = lax.rem(lax.axis_index("row"), CORES)
    copies = []
    for i, (source, side) in enumerate(((got, core), (other, 1 - core))):
        for row in range(nrow):
            start = pl.multiple_of(row % CORES * CORES * tall + side * tall, tall)
            copies.append(
                pltpu.make_async_copy(
                    source.at[pl.ds(row * nstrip, nstrip), pl.ds(0, tall), :],
                    strip.at[:, pl.ds(start, tall), pl.ds(row // CORES * LANES, LANES)],
                    sems.at[i * nrow + row],
                )
            )
    return copies


def scale_kernel(own, nstrip, got, kernels_at, angular_at, scaled, mail, kernels, angular, loads):
    ndev, deep1, _ = got.shape
    nrad = kernels.shape[1]
    parts = nrad // LANES
    rows = mail.shape[1]
    first = [
        pltpu.make_async_copy(got.at[:, pl.ds(deep1 - rows, rows), :], mail, loads.at[0]),
        pltpu.make_async_copy(kernels_at, kernels, loads.at[1]),
        pltpu.make_async_copy(angular_at, angular, loads.at[2]),
    ]
    for copy in first:
        copy.start()
    for copy in first:
        copy.wait()
    mine = jnp.sum(mail[...].astype(F32), axis=0)
    nlam = kernels.shape[0]
    ncoef = angular.shape[0]
    terms = LANES // nstrip
    diagonal = (
        lax.broadcasted_iota(jnp.int32, (nstrip, LANES), 0)
        == lax.broadcasted_iota(jnp.int32, (nstrip, LANES), 1) // terms
    )
    coefs = lax.broadcasted_iota(jnp.int32, (ncoef, LANES), 0).astype(F32)
    lams = lax.broadcasted_iota(jnp.int32, (nlam, LANES), 0).astype(F32)
    lefts, rights, forms = [], [], []
    for a in range(own):
        lam = mine[parts * own + a : parts * own + a + 1, :]
        coef = mine[(parts + 1) * own + a : (parts + 1) * own + a + 1, :]
        value = jnp.sum(jnp.where(coef == coefs, angular[...], 0.0), axis=0, keepdims=True)
        left = jnp.where(diagonal, value, 0.0)
        lefts.append(
            jnp.concatenate([left if b == a else jnp.zeros_like(left) for b in range(own)], axis=1)
        )
        rights.append((lam == lams).astype(F32))
        form = jnp.concatenate([mine[g * own + a : g * own + a + 1, :] for g in range(parts)], axis=1)
        forms.append(jnp.broadcast_to(form, (nstrip, nrad)))
    mixing = lax.dot_general(
        jnp.concatenate(lefts, axis=0),
        jnp.concatenate(rights, axis=1),
        NT,
        precision=lax.Precision.HIGHEST,
        preferred_element_type=F32,
    )
    radial = jnp.dot(mixing, kernels[...], precision=lax.Precision.HIGHEST, preferred_element_type=F32)
    scaled[...] = (jnp.concatenate(forms, axis=0) * radial).astype(BF16)


def chosen_kernel(own, got, other, scaled, kept, second, strip, wave, loads, sent):
    del kept
    nstrip, nmom, nrad = strip.shape
    ndev = got.shape[0]
    copies = strip_copies(got, other, strip, loads)
    for copy in copies:
        copy.start()
    for copy in copies:
        copy.wait()
    scols = nstrip * nmom
    full = lax.dot_general(scaled[...], strip[...].reshape(scols, nrad), NT, preferred_element_type=F32)
    keep = (
        lax.broadcasted_iota(jnp.int32, (nstrip, scols), 0)
        == lax.broadcasted_iota(jnp.int32, (nstrip, scols), 1) // nmom
    )
    chosen = [
        jnp.sum(jnp.where(keep, full[a * nstrip : (a + 1) * nstrip], 0.0), axis=0, keepdims=True) for a in range(own)
    ]
    chosen = jnp.concatenate(chosen, axis=0)
    many, rows, wide = wave.shape
    each = many // CORES
    for core in range(CORES):
        start = core * (scols // CORES)
        cuts = [chosen[:, at : at + wide] for at in range(start, start + scols // CORES, wide)]
        tile = jnp.concatenate(cuts, axis=0).astype(BF16)
        wave[core * each : (core + 1) * each] = jnp.broadcast_to(tile[None], (each,) + wave.shape[1:])
    sends = []
    for g in range(ndev // many):
        send = pltpu.make_async_copy(
            wave, second.at[pl.ds(g * many, many), pl.ds(second.shape[1] - rows, rows), :], sent.at[g]
        )
        send.start()
        sends.append(send)
    for send in sends:
        send.wait()


def assemble_kernel(rows, radial, got, other, lower, out, strip, results, sems, sent):
    group, nrow, nmom, nrad = rows.shape
    nstrip = strip.shape[0]
    npiv = lower.shape[0]
    wide = results.shape[2]
    copies = strip_copies(got, other, strip, sems)
    for copy in copies:
        copy.start()
    low1 = lower[...].astype(BF16)
    low2 = (lower[...] - low1.astype(F32)).astype(BF16)
    for i, low in enumerate((low1, low2)):
        for at in range(0, npiv, wide):
            results[nrow + i, at // wide * npiv : (at // wide + 1) * npiv, :] = low[:, at : at + wide]
    for copy in copies:
        copy.wait()

    def send(p):
        return pltpu.make_async_copy(results.at[p], out.at[p], sent.at[p])

    def one(p, carry):
        forms = [rows[q, p].astype(F32) for q in range(group)]
        for j in range(nstrip):
            scaled = jnp.concatenate(
                [(forms[q] * radial[q, p, j : j + 1, :]).astype(BF16) for q in range(group)], axis=0
            )
            block = lax.dot_general(strip[j], scaled, NT, preferred_element_type=F32)
            results[p, j * nmom : (j + 1) * nmom, :] = block.astype(BF16)
        send(p).start()
        return carry

    send(nrow).start()
    send(nrow + 1).start()
    lax.fori_loop(0, nrow, one, 0)
    for p in range(nrow + 2):
        send(p).wait()


def upper_kernel(own, slot, got, blocks, upper, low1, low2, spread, chosen, low_sems):
    npiv, half = chosen.shape
    ndev, rows, lanes = got.shape[0], spread.shape[0] // got.shape[0], got.shape[2]
    wide = blocks.shape[2]
    lows = []
    for i, low in enumerate((low1, low2)):
        for h in range(npiv // wide):
            lows.append(
                pltpu.make_async_copy(
                    blocks.at[slot + i, pl.ds(h * npiv, npiv), :], low.at[:, pl.ds(h * wide, wide)], low_sems.at[i, h]
                )
            )
    for load in lows:
        load.start()
    spread[...] = got[:, got.shape[1] - rows :, :].astype(F32).reshape(ndev * rows, lanes)
    for g in range(half // lanes):
        for a in range(own):
            chosen[a * ndev : (a + 1) * ndev, g * lanes : (g + 1) * lanes] = spread[
                pl.ds(g * own + a, ndev, stride=rows), :
            ].astype(BF16)
    for load in lows:
        load.wait()
    for at in range(0, half, wide):
        rows_of = chosen[:, at : at + wide]
        part = jnp.dot(low1[...], rows_of, preferred_element_type=F32) + jnp.dot(
            low2[...], rows_of, preferred_element_type=F32
        )
        upper[at : at + wide, :] = part.T.astype(BF16)


def fetch_kernel(blocks, upper, out, sems):
    del upper
    loads = [pltpu.make_async_copy(blocks.at[p], out.at[p], sems.at[p]) for p in range(out.shape[0])]
    for load in loads:
        load.start()
    for load in loads:
        load.wait()


def update_kernel(deep, got, mine, theirs, before, out, upper_t, upper_all):
    nrow, scols, wide = before.shape
    half, npiv = mine.shape
    ncol = npiv // deep
    core = lax.rem(lax.axis_index("row"), CORES)
    upper_all[pl.ds(pl.multiple_of(core * half, half), half), :] = mine[...]
    upper_all[pl.ds(pl.multiple_of((1 - core) * half, half), half), :] = theirs[...]
    width = upper_t.shape[0]
    upper_t[...] = upper_all[pl.ds(pl.multiple_of(lax.axis_index("col") * width, width), width), :]
    for p in range(nrow):
        pieces = [
            got[p * ncol : (p + 1) * ncol, b * deep : (b + 1) * deep, :].reshape(npiv, LANES)
            for b in range(wide // LANES)
        ]
        change = jnp.dot(upper_all[...], jnp.concatenate(pieces, axis=1), preferred_element_type=F32)
        out[p] = (before[p].astype(F32) - change).astype(BF16)


def widen_kernel(got, out, broad, sent):
    ndev, width, wide = got.shape
    steps = sent.shape[0]
    many = ndev // steps
    sends = []
    for s in range(steps):
        for b in range(s * many, (s + 1) * many):
            broad[:, b * wide : (b + 1) * wide] = got[b].astype(F32)
        span = pl.ds(s * many * wide, many * wide)
        send = pltpu.make_async_copy(broad.at[:, span], out.at[:, span], sent.at[s])
        send.start()
        sends.append(send)
    for send in sends:
        send.wait()


def shards(
    form_rows,
    form_strip,
    lam_index,
    coef_index,
    term_count,
    angular_coef,
    kernels,
    pivots,
    lower_inverse,
    panel,
):
    nrow = lax.axis_size("row")
    ncol = lax.axis_size("col")
    ndev = nrow * ncol
    chans, nmom, nrad = form_rows.shape
    nstrip, terms = lam_index.shape[1:]
    nlam = kernels.shape[0]
    npiv = pivots.shape[0]
    scols = nstrip * nmom
    width = scols // ncol
    own = npiv // ndev
    group = chans // nrow
    local = chans * nmom
    vmem = pl.BlockSpec(memory_space=pltpu.VMEM)
    anywhere = pl.BlockSpec(memory_space=pl.ANY)
    dma = pltpu.SemaphoreType.DMA

    tall = nmom // (CORES * CORES)
    extra = 2 * nstrip * terms
    deep1 = tall + own * (nrad + extra) // LANES
    steps, groups = 4, 4
    first = pl.pallas_call(
        functools.partial(pick_kernel, own),
        out_shape=jax.ShapeDtypeStruct((ndev, deep1, LANES), BF16),
        in_specs=[anywhere] * 6,
        out_specs=anywhere,
        scratch_shapes=[
            pltpu.VMEM((1, npiv), jnp.int32),
            pltpu.VMEM((nstrip * terms, chans), jnp.int32),
            pltpu.VMEM((nstrip * terms, chans), jnp.int32),
            pltpu.VMEM((nstrip, chans), jnp.int32),
            pltpu.VMEM(form_strip.shape, BF16),
            pltpu.VMEM((npiv, nrad + extra), F32),
            pltpu.VMEM((steps, local // steps, nrad), BF16),
            pltpu.VMEM((ndev, deep1, LANES), BF16),
            dma((5,)),
            dma((steps,)),
            dma((groups,)),
        ],
        compiler_params=room(56),
        cost_estimate=cost(2 * npiv * local * nrad, 4 << 20),
        name="pick_pivots",
    )(
        pivots[None, :],
        lam_index.transpose(1, 2, 0).reshape(nstrip * terms, chans),
        coef_index.transpose(1, 2, 0).reshape(nstrip * terms, chans),
        term_count.T,
        form_rows.reshape(local, nrad),
        form_strip,
    )
    deep, wide = panel.shape[0], panel.shape[1] // ndev
    flat = deep * wide // LANES
    cut = panel.reshape(deep, ndev, wide // LANES, LANES).transpose(1, 2, 0, 3).reshape(ndev, flat, LANES)
    half = scols // CORES
    wave_rows = own * half // LANES
    second = jnp.pad(cut, ((0, 0), (0, wave_rows), (0, 0)))
    got = exchange(first)
    got, second = lax.optimization_barrier((got, second))
    other = lax.ppermute(got, "row", [(i, i ^ 1) for i in range(nrow)])

    many = 32
    scaled = pl.pallas_call(
        functools.partial(scale_kernel, own, nstrip),
        out_shape=jax.ShapeDtypeStruct((own * nstrip, nrad), BF16),
        in_specs=[anywhere] * 3,
        out_specs=vmem,
        scratch_shapes=[
            pltpu.VMEM((ndev, deep1 - tall, LANES), BF16),
            pltpu.VMEM(kernels.shape, F32),
            pltpu.VMEM((angular_coef.shape[0], 1), F32),
            dma((3,)),
        ],
        compiler_params=room(40),
        cost_estimate=cost(2 * own * nstrip * nrad * LANES, 1 << 20),
        name="scale_pivots",
    )(got, kernels, angular_coef[:, None])
    second = pl.pallas_call(
        functools.partial(chosen_kernel, own),
        out_shape=jax.ShapeDtypeStruct(second.shape, BF16),
        in_specs=[anywhere, anywhere, vmem, anywhere],
        out_specs=anywhere,
        scratch_shapes=[
            pltpu.VMEM((nstrip, nmom, nrad), BF16),
            pltpu.VMEM((many, wave_rows, LANES), BF16),
            dma((CORES * nrow,)),
            dma((ndev // many,)),
        ],
        input_output_aliases={3: 0},
        compiler_params=room(40),
        cost_estimate=cost(2 * own * nstrip * scols * nrad, 4 << 20),
        name="chosen_rows",
    )(got, other, scaled, second)
    got2 = exchange(second)

    position = lax.broadcasted_iota(jnp.int32, lam_index.shape, 2)
    lam = jnp.where(position < term_count[:, :, None], lam_index, nlam)
    mixing = mixing_weights(lam, coef_index, angular_coef, nlam)
    radial = weights_to_radial(mixing, kernels)
    lower = lower_inverse.reshape(npiv, ndev, own).transpose(0, 2, 1).reshape(npiv, npiv)
    slots = 10 * nrow
    blocks = pl.pallas_call(
        assemble_kernel,
        out_shape=jax.ShapeDtypeStruct((slots, scols, group * nmom), BF16),
        in_specs=[vmem, vmem, anywhere, anywhere, vmem],
        out_specs=anywhere,
        scratch_shapes=[
            pltpu.VMEM((nstrip, nmom, nrad), BF16),
            pltpu.VMEM((nrow + 2, scols, group * nmom), BF16),
            dma((CORES * nrow,)),
            dma((nrow + 2,)),
        ],
        compiler_params=room(56),
        cost_estimate=cost(2 * local * scols * nrad * 4, 8 << 20),
        name="assemble_strip",
    )(form_rows.reshape(group, nrow, nmom, nrad), radial.reshape(group, nrow, nstrip, nrad), got, other, lower)

    mine = pl.pallas_call(
        functools.partial(upper_kernel, own, nrow),
        out_shape=jax.ShapeDtypeStruct((half, npiv), BF16),
        in_specs=[vmem, anywhere],
        out_specs=vmem,
        scratch_shapes=[
            pltpu.VMEM((npiv, npiv), BF16),
            pltpu.VMEM((npiv, npiv), BF16),
            pltpu.VMEM((ndev * wave_rows, LANES), F32),
            pltpu.VMEM((npiv, half), BF16),
            dma((2, npiv // wide)),
        ],
        compiler_params=room(24),
        cost_estimate=cost(4 * npiv * npiv * half, 2 << 20),
        name="upper_rows",
    )(got2, blocks)
    theirs = lax.ppermute(mine, "row", [(i, i ^ 1) for i in range(nrow)])
    fetched = pl.pallas_call(
        fetch_kernel,
        out_shape=jax.ShapeDtypeStruct((nrow, scols, wide), BF16),
        in_specs=[anywhere, anywhere],
        out_specs=vmem,
        scratch_shapes=[dma((nrow,))],
        compiler_params=room(16),
        cost_estimate=cost(0, 8 << 20),
        name="fetch_blocks",
    )(blocks, mine)
    done, upper_t = pl.pallas_call(
        functools.partial(update_kernel, deep),
        out_shape=(
            jax.ShapeDtypeStruct((nrow, scols, wide), BF16),
            jax.ShapeDtypeStruct((width, npiv), BF16),
        ),
        in_specs=[vmem, vmem, vmem, vmem],
        out_specs=(vmem, vmem),
        scratch_shapes=[pltpu.VMEM((scols, npiv), BF16)],
        compiler_params=room(16),
        cost_estimate=cost(2 * npiv * scols * local, 12 << 20),
        name="update_blocks",
    )(got2, mine, theirs, fetched)
    final = exchange(done.reshape(ndev, width, wide))
    steps = 16
    trailing = pl.pallas_call(
        widen_kernel,
        out_shape=jax.ShapeDtypeStruct((width, ndev * wide), F32),
        in_specs=[vmem],
        out_specs=anywhere,
        scratch_shapes=[pltpu.VMEM((width, ndev * wide), F32), dma((steps,))],
        compiler_params=room(20),
        cost_estimate=cost(ndev * width * wide, 12 << 20),
        name="widen_blocks",
    )(final)
    return (trailing, upper_t)


def solution(mesh):
    in_specs = (
        P(("row", "col"), None, None),
        P("col", None, None),
        P(("row", "col"), None, None),
        P(("row", "col"), None, None),
        P(("row", "col"), None),
        P(),
        P(),
        P(),
        P(),
        P("col", "row"),
    )
    out_specs = (P("col", "row"), P("col", None))
    return jax.shard_map(shards, mesh=mesh, in_specs=in_specs, out_specs=out_specs, check_vma=False)
```

```python
import functools

import jax
import jax.numpy as jnp
from jax import lax
from jax.experimental import pallas as pl
from jax.experimental.pallas import tpu as pltpu
from jax.sharding import PartitionSpec as P

ALL = ("row", "col")
LANES = 128
CORES = 2
BF16, F32 = jnp.bfloat16, jnp.float32
NT = (((1,), (1,)), ((), ()))


def room(mebibytes):
    return pltpu.CompilerParams(vmem_limit_bytes=mebibytes * 1024 * 1024)


def exchange(chunks):
    return lax.all_to_all(chunks, ALL, split_axis=0, concat_axis=0, tiled=True)


def cost(flops, bytes_accessed):
    return pl.CostEstimate(flops=flops, bytes_accessed=bytes_accessed, transcendentals=0)


def mixing_weights(lam, coef, angular_coef, nlam):
    coef_table = (coef[..., None] == jnp.arange(angular_coef.shape[0], dtype=coef.dtype)).astype(F32)
    coef_value = jnp.sum(coef_table * angular_coef, axis=-1)
    lam_table = (lam[..., None] == jnp.arange(nlam, dtype=lam.dtype)).astype(F32)
    return jnp.sum(coef_value[..., None] * lam_table, axis=-2)


def weights_to_radial(mixing, kernels):
    chans, strips, nlam = mixing.shape
    radial = jnp.dot(mixing.reshape(chans * strips, nlam), kernels, precision=lax.Precision.HIGHEST)
    return radial.reshape(chans, strips, kernels.shape[1])


def pick_kernel(
    own,
    pivots_at,
    lam_at,
    coef_at,
    count_at,
    rows,
    form_strip_at,
    out,
    pivots,
    lam,
    coef,
    count,
    form_strip,
    acc,
    pieces,
    chunks,
    small,
    sems,
    done,
):
    pairs = ((form_strip_at, form_strip), (pivots_at, pivots), (lam_at, lam), (coef_at, coef), (count_at, count))
    loads = [pltpu.make_async_copy(source, target, small.at[i]) for i, (source, target) in enumerate(pairs)]
    for load in loads:
        load.start()
    npiv = pivots.shape[1]
    local, nrad = rows.shape
    nstrip, chans = count.shape
    terms = lam.shape[0] // nstrip
    nmom = local // chans
    steps = sems.shape[0]
    depth = local // steps
    ndev, deep1, _ = out.shape
    copies = [
        pltpu.make_async_copy(rows.at[pl.ds(s * depth, depth), :], pieces.at[s], sems.at[s]) for s in range(steps)
    ]
    for copy in copies:
        copy.start()
    row = lax.axis_index("row")
    me = row * lax.axis_size("col") + lax.axis_index("col")
    for load in loads:
        load.wait()
    tall = deep1 - own * acc.shape[1] // LANES
    ncol = lax.axis_size("col")
    half, part = lax.rem(row, CORES), lax.div(row, CORES)
    for core in range(CORES):
        start = half * CORES * tall + core * tall
        share = form_strip[
            0,
            pl.ds(pl.multiple_of(start, tall), tall),
            pl.ds(pl.multiple_of(part * LANES, LANES), LANES),
        ]
        for at in range(core * ncol, ndev, CORES * ncol):
            chunks[at : at + ncol, :tall, :] = jnp.broadcast_to(share[None], (ncol, tall, LANES))
    column = jnp.broadcast_to(pivots[...].astype(F32), (LANES, npiv)).T[:, :1].astype(jnp.int32) - me * local
    counts = jnp.broadcast_to(count[...][:, None, :], (nstrip, terms, chans)).reshape(nstrip * terms, chans)
    position = lax.rem(lax.broadcasted_iota(jnp.int32, (nstrip * terms, chans), 0), terms)
    order = jnp.where(position < counts, lam[...], LANES)
    table = jnp.concatenate([order, coef[...]], axis=0).astype(F32).astype(BF16)
    first = lax.broadcasted_iota(jnp.int32, (npiv, chans), 1) * nmom
    pick = jnp.logical_and(column >= first, column < first + nmom).astype(F32).astype(BF16)
    acc[:, nrad:] = lax.dot_general(pick, table, NT, preferred_element_type=F32)
    total = None
    for s in range(steps):
        pick = (column - s * depth == lax.broadcasted_iota(jnp.int32, (npiv, depth), 1)).astype(F32).astype(BF16)
        copies[s].wait()
        part = jnp.dot(pick, pieces[s], preferred_element_type=F32)
        total = part if total is None else total + part
    acc[:, :nrad] = total
    groups = done.shape[0]
    per = ndev // groups
    low = lax.broadcasted_iota(jnp.int32, (per // 2, 2 * own, LANES), 1) < own
    sends = []
    for g in range(groups):
        tiles = []
        for at in range(0, acc.shape[1], 2 * LANES):
            left = acc[g * per * own : (g + 1) * per * own, at : at + LANES].reshape(per // 2, 2 * own, LANES)
            right = acc[g * per * own : (g + 1) * per * own, at + LANES : at + 2 * LANES].reshape(
                per // 2, 2 * own, LANES
            )
            even = jnp.where(low, left, pltpu.roll(right, own, 1))
            odd = jnp.where(low, pltpu.roll(left, own, 1), right)
            tiles.append(jnp.stack([even, odd], axis=1).reshape(per, 2 * own, LANES))
        chunks[g * per : (g + 1) * per, tall:, :] = jnp.concatenate(tiles, axis=1).astype(BF16)
        send = pltpu.make_async_copy(chunks.at[pl.ds(g * per, per)], out.at[pl.ds(g * per, per)], done.at[g])
        send.start()
        sends.append(send)
    for send in sends:
        send.wait()


def strip_copies(got, other, strip, sems):
    nstrip, nmom, nrad = strip.shape
    nrow = got.shape[0] // nstrip
    tall = nmom // (CORES * CORES)
    core = lax.rem(lax.axis_index("row"), CORES)
    copies = []
    for i, (source, side) in enumerate(((got, core), (other, 1 - core))):
        for row in range(nrow):
            start = pl.multiple_of(row % CORES * CORES * tall + side * tall, tall)
            copies.append(
                pltpu.make_async_copy(
                    source.at[pl.ds(row * nstrip, nstrip), pl.ds(0, tall), :],
                    strip.at[:, pl.ds(start, tall), pl.ds(row // CORES * LANES, LANES)],
                    sems.at[i * nrow + row],
                )
            )
    return copies


def scale_kernel(own, nstrip, got, kernels_at, angular_at, scaled, mail, kernels, angular, loads):
    ndev, deep1, _ = got.shape
    nrad = kernels.shape[1]
    parts = nrad // LANES
    rows = mail.shape[1]
    first = [
        pltpu.make_async_copy(got.at[:, pl.ds(deep1 - rows, rows), :], mail, loads.at[0]),
        pltpu.make_async_copy(kernels_at, kernels, loads.at[1]),
        pltpu.make_async_copy(angular_at, angular, loads.at[2]),
    ]
    for copy in first:
        copy.start()
    for copy in first:
        copy.wait()
    mine = jnp.sum(mail[...].astype(F32), axis=0)
    nlam = kernels.shape[0]
    ncoef = angular.shape[0]
    terms = LANES // nstrip
    diagonal = (
        lax.broadcasted_iota(jnp.int32, (nstrip, LANES), 0)
        == lax.broadcasted_iota(jnp.int32, (nstrip, LANES), 1) // terms
    )
    coefs = lax.broadcasted_iota(jnp.int32, (ncoef, LANES), 0).astype(F32)
    lams = lax.broadcasted_iota(jnp.int32, (nlam, LANES), 0).astype(F32)
    lefts, rights, forms = [], [], []
    for a in range(own):
        lam = mine[parts * own + a : parts * own + a + 1, :]
        coef = mine[(parts + 1) * own + a : (parts + 1) * own + a + 1, :]
        value = jnp.sum(jnp.where(coef == coefs, angular[...], 0.0), axis=0, keepdims=True)
        left = jnp.where(diagonal, value, 0.0)
        lefts.append(
            jnp.concatenate([left if b == a else jnp.zeros_like(left) for b in range(own)], axis=1)
        )
        rights.append((lam == lams).astype(F32))
        form = jnp.concatenate([mine[g * own + a : g * own + a + 1, :] for g in range(parts)], axis=1)
        forms.append(jnp.broadcast_to(form, (nstrip, nrad)))
    mixing = lax.dot_general(
        jnp.concatenate(lefts, axis=0),
        jnp.concatenate(rights, axis=1),
        NT,
        precision=lax.Precision.HIGHEST,
        preferred_element_type=F32,
    )
    radial = jnp.dot(mixing, kernels[...], precision=lax.Precision.HIGHEST, preferred_element_type=F32)
    scaled[...] = (jnp.concatenate(forms, axis=0) * radial).astype(BF16)


def chosen_kernel(own, got, other, scaled, kept, second, strip, wave, loads, sent):
    del kept
    nstrip, nmom, nrad = strip.shape
    ndev = got.shape[0]
    copies = strip_copies(got, other, strip, loads)
    for copy in copies:
        copy.start()
    for copy in copies:
        copy.wait()
    scols = nstrip * nmom
    full = lax.dot_general(scaled[...], strip[...].reshape(scols, nrad), NT, preferred_element_type=F32)
    keep = (
        lax.broadcasted_iota(jnp.int32, (nstrip, scols), 0)
        == lax.broadcasted_iota(jnp.int32, (nstrip, scols), 1) // nmom
    )
    chosen = [
        jnp.sum(jnp.where(keep, full[a * nstrip : (a + 1) * nstrip], 0.0), axis=0, keepdims=True) for a in range(own)
    ]
    chosen = jnp.concatenate(chosen, axis=0)
    many, rows, wide = wave.shape
    each = many // CORES
    for core in range(CORES):
        start = core * (scols // CORES)
        cuts = [chosen[:, at : at + wide] for at in range(start, start + scols // CORES, wide)]
        tile = jnp.concatenate(cuts, axis=0).astype(BF16)
        wave[core * each : (core + 1) * each] = jnp.broadcast_to(tile[None], (each,) + wave.shape[1:])
    sends = []
    for g in range(ndev // many):
        send = pltpu.make_async_copy(
            wave, second.at[pl.ds(g * many, many), pl.ds(second.shape[1] - rows, rows), :], sent.at[g]
        )
        send.start()
        sends.append(send)
    for send in sends:
        send.wait()


def assemble_kernel(rows, radial, got, other, lower, out, strip, results, sems, sent):
    group, nrow, nmom, nrad = rows.shape
    nstrip = strip.shape[0]
    npiv = lower.shape[0]
    wide = results.shape[2]
    copies = strip_copies(got, other, strip, sems)
    for copy in copies:
        copy.start()
    low1 = lower[...].astype(BF16)
    low2 = (lower[...] - low1.astype(F32)).astype(BF16)
    for i, low in enumerate((low1, low2)):
        for at in range(0, npiv, wide):
            results[nrow + i, at // wide * npiv : (at // wide + 1) * npiv, :] = low[:, at : at + wide]
    for copy in copies:
        copy.wait()

    def send(p):
        return pltpu.make_async_copy(results.at[p], out.at[p], sent.at[p])

    def one(p, carry):
        forms = [rows[q, p].astype(F32) for q in range(group)]
        for j in range(nstrip):
            scaled = jnp.concatenate(
                [(forms[q] * radial[q, p, j : j + 1, :]).astype(BF16) for q in range(group)], axis=0
            )
            block = lax.dot_general(strip[j], scaled, NT, preferred_element_type=F32)
            results[p, j * nmom : (j + 1) * nmom, :] = block.astype(BF16)
        send(p).start()
        return carry

    send(nrow).start()
    send(nrow + 1).start()
    lax.fori_loop(0, nrow, one, 0)
    for p in range(nrow + 2):
        send(p).wait()


def upper_kernel(own, slot, got, blocks, upper, low1, low2, spread, chosen, low_sems):
    npiv, half = chosen.shape
    ndev, rows, lanes = got.shape[0], spread.shape[0] // got.shape[0], got.shape[2]
    wide = blocks.shape[2]
    lows = []
    for i, low in enumerate((low1, low2)):
        for h in range(npiv // wide):
            lows.append(
                pltpu.make_async_copy(
                    blocks.at[slot + i, pl.ds(h * npiv, npiv), :], low.at[:, pl.ds(h * wide, wide)], low_sems.at[i, h]
                )
            )
    for load in lows:
        load.start()
    spread[...] = got[:, got.shape[1] - rows :, :].astype(F32).reshape(ndev * rows, lanes)
    for g in range(half // lanes):
        for a in range(own):
            chosen[a * ndev : (a + 1) * ndev, g * lanes : (g + 1) * lanes] = spread[
                pl.ds(g * own + a, ndev, stride=rows), :
            ].astype(BF16)
    each = npiv // wide
    for load in lows[:each]:
        load.wait()
    parts = [
        jnp.dot(low1[...], chosen[:, at : at + wide], preferred_element_type=F32) for at in range(0, half, wide)
    ]
    for load in lows[each:]:
        load.wait()
    for i, part in enumerate(parts):
        span = slice(i * wide, (i + 1) * wide)
        part = part + jnp.dot(low2[...], chosen[:, span], preferred_element_type=F32)
        upper[span, :] = part.T.astype(BF16)


def fetch_kernel(blocks, upper, out, sems):
    del upper
    loads = [pltpu.make_async_copy(blocks.at[p], out.at[p], sems.at[p]) for p in range(out.shape[0])]
    for load in loads:
        load.start()
    for load in loads:
        load.wait()


def update_kernel(deep, got, mine, theirs, before, out, upper_t, upper_all):
    nrow, scols, wide = before.shape
    half, npiv = mine.shape
    ncol = npiv // deep
    core = lax.rem(lax.axis_index("row"), CORES)
    upper_all[pl.ds(pl.multiple_of(core * half, half), half), :] = mine[...]
    upper_all[pl.ds(pl.multiple_of((1 - core) * half, half), half), :] = theirs[...]
    width = upper_t.shape[0]
    upper_t[...] = upper_all[pl.ds(pl.multiple_of(lax.axis_index("col") * width, width), width), :]
    for p in range(nrow):
        pieces = [
            got[p * ncol : (p + 1) * ncol, b * deep : (b + 1) * deep, :].reshape(npiv, LANES)
            for b in range(wide // LANES)
        ]
        change = jnp.dot(upper_all[...], jnp.concatenate(pieces, axis=1), preferred_element_type=F32)
        out[p] = (before[p].astype(F32) - change).astype(BF16)


def widen_kernel(got, out, broad, sent):
    ndev, width, wide = got.shape
    steps = sent.shape[0]
    many = ndev // steps
    sends = []
    for s in range(steps):
        for b in range(s * many, (s + 1) * many):
            broad[:, b * wide : (b + 1) * wide] = got[b].astype(F32)
        span = pl.ds(s * many * wide, many * wide)
        send = pltpu.make_async_copy(broad.at[:, span], out.at[:, span], sent.at[s])
        send.start()
        sends.append(send)
    for send in sends:
        send.wait()


def shards(
    form_rows,
    form_strip,
    lam_index,
    coef_index,
    term_count,
    angular_coef,
    kernels,
    pivots,
    lower_inverse,
    panel,
):
    nrow = lax.axis_size("row")
    ncol = lax.axis_size("col")
    ndev = nrow * ncol
    chans, nmom, nrad = form_rows.shape
    nstrip, terms = lam_index.shape[1:]
    nlam = kernels.shape[0]
    npiv = pivots.shape[0]
    scols = nstrip * nmom
    width = scols // ncol
    own = npiv // ndev
    group = chans // nrow
    local = chans * nmom
    vmem = pl.BlockSpec(memory_space=pltpu.VMEM)
    anywhere = pl.BlockSpec(memory_space=pl.ANY)
    dma = pltpu.SemaphoreType.DMA

    tall = nmom // (CORES * CORES)
    extra = 2 * nstrip * terms
    deep1 = tall + own * (nrad + extra) // LANES
    steps, groups = 2, 4
    first = pl.pallas_call(
        functools.partial(pick_kernel, own),
        out_shape=jax.ShapeDtypeStruct((ndev, deep1, LANES), BF16),
        in_specs=[anywhere] * 6,
        out_specs=anywhere,
        scratch_shapes=[
            pltpu.VMEM((1, npiv), jnp.int32),
            pltpu.VMEM((nstrip * terms, chans), jnp.int32),
            pltpu.VMEM((nstrip * terms, chans), jnp.int32),
            pltpu.VMEM((nstrip, chans), jnp.int32),
            pltpu.VMEM(form_strip.shape, BF16),
            pltpu.VMEM((npiv, nrad + extra), F32),
            pltpu.VMEM((steps, local // steps, nrad), BF16),
            pltpu.VMEM((ndev, deep1, LANES), BF16),
            dma((5,)),
            dma((steps,)),
            dma((groups,)),
        ],
        compiler_params=room(56),
        cost_estimate=cost(2 * npiv * local * nrad, 4 << 20),
        name="pick_pivots",
    )(
        pivots[None, :],
        lam_index.transpose(1, 2, 0).reshape(nstrip * terms, chans),
        coef_index.transpose(1, 2, 0).reshape(nstrip * terms, chans),
        term_count.T,
        form_rows.reshape(local, nrad),
        form_strip,
    )
    deep, wide = panel.shape[0], panel.shape[1] // ndev
    flat = deep * wide // LANES
    cut = panel.reshape(deep, ndev, wide // LANES, LANES).transpose(1, 2, 0, 3).reshape(ndev, flat, LANES)
    half = scols // CORES
    wave_rows = own * half // LANES
    second = jnp.pad(cut, ((0, 0), (0, wave_rows), (0, 0)))
    got = exchange(first)
    got, second = lax.optimization_barrier((got, second))
    other = lax.ppermute(got, "row", [(i, i ^ 1) for i in range(nrow)])

    many = 32
    scaled = pl.pallas_call(
        functools.partial(scale_kernel, own, nstrip),
        out_shape=jax.ShapeDtypeStruct((own * nstrip, nrad), BF16),
        in_specs=[anywhere] * 3,
        out_specs=vmem,
        scratch_shapes=[
            pltpu.VMEM((ndev, deep1 - tall, LANES), BF16),
            pltpu.VMEM(kernels.shape, F32),
            pltpu.VMEM((angular_coef.shape[0], 1), F32),
            dma((3,)),
        ],
        compiler_params=room(40),
        cost_estimate=cost(2 * own * nstrip * nrad * LANES, 1 << 20),
        name="scale_pivots",
    )(got, kernels, angular_coef[:, None])
    second = pl.pallas_call(
        functools.partial(chosen_kernel, own),
        out_shape=jax.ShapeDtypeStruct(second.shape, BF16),
        in_specs=[anywhere, anywhere, vmem, anywhere],
        out_specs=anywhere,
        scratch_shapes=[
            pltpu.VMEM((nstrip, nmom, nrad), BF16),
            pltpu.VMEM((many, wave_rows, LANES), BF16),
            dma((CORES * nrow,)),
            dma((ndev // many,)),
        ],
        input_output_aliases={3: 0},
        compiler_params=room(40),
        cost_estimate=cost(2 * own * nstrip * scols * nrad, 4 << 20),
        name="chosen_rows",
    )(got, other, scaled, second)
    got2 = exchange(second)

    position = lax.broadcasted_iota(jnp.int32, lam_index.shape, 2)
    lam = jnp.where(position < term_count[:, :, None], lam_index, nlam)
    mixing = mixing_weights(lam, coef_index, angular_coef, nlam)
    radial = weights_to_radial(mixing, kernels)
    lower = lower_inverse.reshape(npiv, ndev, own).transpose(0, 2, 1).reshape(npiv, npiv)
    slots = 10 * nrow
    blocks = pl.pallas_call(
        assemble_kernel,
        out_shape=jax.ShapeDtypeStruct((slots, scols, group * nmom), BF16),
        in_specs=[vmem, vmem, anywhere, anywhere, vmem],
        out_specs=anywhere,
        scratch_shapes=[
            pltpu.VMEM((nstrip, nmom, nrad), BF16),
            pltpu.VMEM((nrow + 2, scols, group * nmom), BF16),
            dma((CORES * nrow,)),
            dma((nrow + 2,)),
        ],
        compiler_params=room(56),
        cost_estimate=cost(2 * local * scols * nrad * 4, 8 << 20),
        name="assemble_strip",
    )(form_rows.reshape(group, nrow, nmom, nrad), radial.reshape(group, nrow, nstrip, nrad), got, other, lower)

    mine = pl.pallas_call(
        functools.partial(upper_kernel, own, nrow),
        out_shape=jax.ShapeDtypeStruct((half, npiv), BF16),
        in_specs=[vmem, anywhere],
        out_specs=vmem,
        scratch_shapes=[
            pltpu.VMEM((npiv, npiv), BF16),
            pltpu.VMEM((npiv, npiv), BF16),
            pltpu.VMEM((ndev * wave_rows, LANES), F32),
            pltpu.VMEM((npiv, half), BF16),
            dma((2, npiv // wide)),
        ],
        compiler_params=room(24),
        cost_estimate=cost(4 * npiv * npiv * half, 2 << 20),
        name="upper_rows",
    )(got2, blocks)
    theirs = lax.ppermute(mine, "row", [(i, i ^ 1) for i in range(nrow)])
    fetched = pl.pallas_call(
        fetch_kernel,
        out_shape=jax.ShapeDtypeStruct((nrow, scols, wide), BF16),
        in_specs=[anywhere, anywhere],
        out_specs=vmem,
        scratch_shapes=[dma((nrow,))],
        compiler_params=room(16),
        cost_estimate=cost(0, 8 << 20),
        name="fetch_blocks",
    )(blocks, mine)
    done, upper_t = pl.pallas_call(
        functools.partial(update_kernel, deep),
        out_shape=(
            jax.ShapeDtypeStruct((nrow, scols, wide), BF16),
            jax.ShapeDtypeStruct((width, npiv), BF16),
        ),
        in_specs=[vmem, vmem, vmem, vmem],
        out_specs=(vmem, vmem),
        scratch_shapes=[pltpu.VMEM((scols, npiv), BF16)],
        compiler_params=room(16),
        cost_estimate=cost(2 * npiv * scols * local, 12 << 20),
        name="update_blocks",
    )(got2, mine, theirs, fetched)
    final = exchange(done.reshape(ndev, width, wide))
    steps = 8
    trailing = pl.pallas_call(
        widen_kernel,
        out_shape=jax.ShapeDtypeStruct((width, ndev * wide), F32),
        in_specs=[vmem],
        out_specs=anywhere,
        scratch_shapes=[pltpu.VMEM((width, ndev * wide), F32), dma((steps,))],
        compiler_params=room(20),
        cost_estimate=cost(ndev * width * wide, 12 << 20),
        name="widen_blocks",
    )(final)
    return (trailing, upper_t)


def solution(mesh):
    in_specs = (
        P(("row", "col"), None, None),
        P("col", None, None),
        P(("row", "col"), None, None),
        P(("row", "col"), None, None),
        P(("row", "col"), None),
        P(),
        P(),
        P(),
        P(),
        P("col", "row"),
    )
    out_specs = (P("col", "row"), P("col", None))
    return jax.shard_map(shards, mesh=mesh, in_specs=in_specs, out_specs=out_specs, check_vma=False)
```

```python
import functools

import jax
import jax.numpy as jnp
from jax import lax
from jax.experimental import pallas as pl
from jax.experimental.pallas import tpu as pltpu
from jax.sharding import PartitionSpec as P

ALL = ("row", "col")
LANES = 128
CORES = 2
BF16, F32 = jnp.bfloat16, jnp.float32
NT = (((1,), (1,)), ((), ()))


def room(mebibytes):
    return pltpu.CompilerParams(vmem_limit_bytes=mebibytes * 1024 * 1024)


def exchange(chunks):
    return lax.all_to_all(chunks, ALL, split_axis=0, concat_axis=0, tiled=True)


def cost(flops, bytes_accessed):
    return pl.CostEstimate(flops=flops, bytes_accessed=bytes_accessed, transcendentals=0)


def mixing_weights(lam, coef, angular_coef, nlam):
    coef_table = (coef[..., None] == jnp.arange(angular_coef.shape[0], dtype=coef.dtype)).astype(F32)
    coef_value = jnp.sum(coef_table * angular_coef, axis=-1)
    lam_table = (lam[..., None] == jnp.arange(nlam, dtype=lam.dtype)).astype(F32)
    return jnp.sum(coef_value[..., None] * lam_table, axis=-2)


def weights_to_radial(mixing, kernels):
    chans, strips, nlam = mixing.shape
    radial = jnp.dot(mixing.reshape(chans * strips, nlam), kernels, precision=lax.Precision.HIGHEST)
    return radial.reshape(chans, strips, kernels.shape[1])


def pick_kernel(
    own,
    pivots_at,
    lam_at,
    coef_at,
    count_at,
    rows,
    form_strip_at,
    out,
    pivots,
    lam,
    coef,
    count,
    form_strip,
    acc,
    pieces,
    chunks,
    small,
    sems,
    done,
):
    pairs = ((form_strip_at, form_strip), (pivots_at, pivots), (lam_at, lam), (coef_at, coef), (count_at, count))
    loads = [pltpu.make_async_copy(source, target, small.at[i]) for i, (source, target) in enumerate(pairs)]
    for load in loads:
        load.start()
    npiv = pivots.shape[1]
    local, nrad = rows.shape
    nstrip, chans = count.shape
    terms = lam.shape[0] // nstrip
    nmom = local // chans
    steps = sems.shape[0]
    depth = local // steps
    ndev, deep1, _ = out.shape
    copies = [
        pltpu.make_async_copy(rows.at[pl.ds(s * depth, depth), :], pieces.at[s], sems.at[s]) for s in range(steps)
    ]
    for copy in copies:
        copy.start()
    row = lax.axis_index("row")
    me = row * lax.axis_size("col") + lax.axis_index("col")
    for load in loads:
        load.wait()
    tall = deep1 - own * acc.shape[1] // LANES
    ncol = lax.axis_size("col")
    half, part = lax.rem(row, CORES), lax.div(row, CORES)
    for core in range(CORES):
        start = half * CORES * tall + core * tall
        share = form_strip[
            0,
            pl.ds(pl.multiple_of(start, tall), tall),
            pl.ds(pl.multiple_of(part * LANES, LANES), LANES),
        ]
        for at in range(core * ncol, ndev, CORES * ncol):
            chunks[at : at + ncol, :tall, :] = jnp.broadcast_to(share[None], (ncol, tall, LANES))
    column = jnp.broadcast_to(pivots[...].astype(F32), (LANES, npiv)).T[:, :1].astype(jnp.int32) - me * local
    counts = jnp.broadcast_to(count[...][:, None, :], (nstrip, terms, chans)).reshape(nstrip * terms, chans)
    position = lax.rem(lax.broadcasted_iota(jnp.int32, (nstrip * terms, chans), 0), terms)
    order = jnp.where(position < counts, lam[...], LANES)
    table = jnp.concatenate([order, coef[...]], axis=0).astype(F32).astype(BF16)
    first = lax.broadcasted_iota(jnp.int32, (npiv, chans), 1) * nmom
    pick = jnp.logical_and(column >= first, column < first + nmom).astype(F32).astype(BF16)
    acc[:, nrad:] = lax.dot_general(pick, table, NT, preferred_element_type=F32)
    total = None
    for s in range(steps):
        pick = (column - s * depth == lax.broadcasted_iota(jnp.int32, (npiv, depth), 1)).astype(F32).astype(BF16)
        copies[s].wait()
        part = jnp.dot(pick, pieces[s], preferred_element_type=F32)
        total = part if total is None else total + part
    acc[:, :nrad] = total
    groups = done.shape[0]
    per = ndev // groups
    low = lax.broadcasted_iota(jnp.int32, (per // 2, 2 * own, LANES), 1) < own
    sends = []
    for g in range(groups):
        tiles = []
        for at in range(0, acc.shape[1], 2 * LANES):
            left = acc[g * per * own : (g + 1) * per * own, at : at + LANES].reshape(per // 2, 2 * own, LANES)
            right = acc[g * per * own : (g + 1) * per * own, at + LANES : at + 2 * LANES].reshape(
                per // 2, 2 * own, LANES
            )
            even = jnp.where(low, left, pltpu.roll(right, own, 1))
            odd = jnp.where(low, pltpu.roll(left, own, 1), right)
            tiles.append(jnp.stack([even, odd], axis=1).reshape(per, 2 * own, LANES))
        chunks[g * per : (g + 1) * per, tall:, :] = jnp.concatenate(tiles, axis=1).astype(BF16)
        send = pltpu.make_async_copy(chunks.at[pl.ds(g * per, per)], out.at[pl.ds(g * per, per)], done.at[g])
        send.start()
        sends.append(send)
    for send in sends:
        send.wait()


def strip_copies(got, other, strip, sems):
    nstrip, nmom, nrad = strip.shape
    nrow = got.shape[0] // nstrip
    tall = nmom // (CORES * CORES)
    core = lax.rem(lax.axis_index("row"), CORES)
    copies = []
    for i, (source, side) in enumerate(((got, core), (other, 1 - core))):
        for row in range(nrow):
            start = pl.multiple_of(row % CORES * CORES * tall + side * tall, tall)
            copies.append(
                pltpu.make_async_copy(
                    source.at[pl.ds(row * nstrip, nstrip), pl.ds(0, tall), :],
                    strip.at[:, pl.ds(start, tall), pl.ds(row // CORES * LANES, LANES)],
                    sems.at[i * nrow + row],
                )
            )
    return copies


def scale_kernel(own, nstrip, got, kernels_at, angular_at, scaled, mail, kernels, angular, loads):
    ndev, deep1, _ = got.shape
    nrad = kernels.shape[1]
    parts = nrad // LANES
    rows = mail.shape[1]
    first = [
        pltpu.make_async_copy(got.at[:, pl.ds(deep1 - rows, rows), :], mail, loads.at[0]),
        pltpu.make_async_copy(kernels_at, kernels, loads.at[1]),
        pltpu.make_async_copy(angular_at, angular, loads.at[2]),
    ]
    for copy in first:
        copy.start()
    for copy in first:
        copy.wait()
    mine = jnp.sum(mail[...].astype(F32), axis=0)
    nlam = kernels.shape[0]
    ncoef = angular.shape[0]
    terms = LANES // nstrip
    diagonal = (
        lax.broadcasted_iota(jnp.int32, (nstrip, LANES), 0)
        == lax.broadcasted_iota(jnp.int32, (nstrip, LANES), 1) // terms
    )
    coefs = lax.broadcasted_iota(jnp.int32, (ncoef, LANES), 0).astype(F32)
    lams = lax.broadcasted_iota(jnp.int32, (nlam, LANES), 0).astype(F32)
    lefts, rights, forms = [], [], []
    for a in range(own):
        lam = mine[parts * own + a : parts * own + a + 1, :]
        coef = mine[(parts + 1) * own + a : (parts + 1) * own + a + 1, :]
        value = jnp.sum(jnp.where(coef == coefs, angular[...], 0.0), axis=0, keepdims=True)
        left = jnp.where(diagonal, value, 0.0)
        lefts.append(
            jnp.concatenate([left if b == a else jnp.zeros_like(left) for b in range(own)], axis=1)
        )
        rights.append((lam == lams).astype(F32))
        form = jnp.concatenate([mine[g * own + a : g * own + a + 1, :] for g in range(parts)], axis=1)
        forms.append(jnp.broadcast_to(form, (nstrip, nrad)))
    mixing = lax.dot_general(
        jnp.concatenate(lefts, axis=0),
        jnp.concatenate(rights, axis=1),
        NT,
        precision=lax.Precision.HIGHEST,
        preferred_element_type=F32,
    )
    radial = jnp.dot(mixing, kernels[...], precision=lax.Precision.HIGHEST, preferred_element_type=F32)
    scaled[...] = (jnp.concatenate(forms, axis=0) * radial).astype(BF16)


def chosen_kernel(own, got, other, scaled, kept, second, strip, wave, loads, sent):
    del kept
    nstrip, nmom, nrad = strip.shape
    ndev = got.shape[0]
    copies = strip_copies(got, other, strip, loads)
    for copy in copies:
        copy.start()
    for copy in copies:
        copy.wait()
    scols = nstrip * nmom
    full = lax.dot_general(scaled[...], strip[...].reshape(scols, nrad), NT, preferred_element_type=F32)
    keep = (
        lax.broadcasted_iota(jnp.int32, (nstrip, scols), 0)
        == lax.broadcasted_iota(jnp.int32, (nstrip, scols), 1) // nmom
    )
    chosen = [
        jnp.sum(jnp.where(keep, full[a * nstrip : (a + 1) * nstrip], 0.0), axis=0, keepdims=True) for a in range(own)
    ]
    chosen = jnp.concatenate(chosen, axis=0)
    many, rows, wide = wave.shape
    each = many // CORES
    for core in range(CORES):
        start = core * (scols // CORES)
        cuts = [chosen[:, at : at + wide] for at in range(start, start + scols // CORES, wide)]
        tile = jnp.concatenate(cuts, axis=0).astype(BF16)
        wave[core * each : (core + 1) * each] = jnp.broadcast_to(tile[None], (each,) + wave.shape[1:])
    sends = []
    for g in range(ndev // many):
        send = pltpu.make_async_copy(
            wave, second.at[pl.ds(g * many, many), pl.ds(second.shape[1] - rows, rows), :], sent.at[g]
        )
        send.start()
        sends.append(send)
    for send in sends:
        send.wait()


def assemble_kernel(rows, radial, got, other, lower, out, strip, results, sems, sent):
    group, nrow, nmom, nrad = rows.shape
    nstrip = strip.shape[0]
    npiv = lower.shape[0]
    wide = results.shape[2]
    copies = strip_copies(got, other, strip, sems)
    for copy in copies:
        copy.start()
    low1 = lower[...].astype(BF16)
    low2 = (lower[...] - low1.astype(F32)).astype(BF16)
    for i, low in enumerate((low1, low2)):
        for at in range(0, npiv, wide):
            results[nrow + i, at // wide * npiv : (at // wide + 1) * npiv, :] = low[:, at : at + wide]
    for copy in copies:
        copy.wait()

    def send(p):
        return pltpu.make_async_copy(results.at[p], out.at[p], sent.at[p])

    def one(p, carry):
        forms = [rows[q, p].astype(F32) for q in range(group)]
        for j in range(nstrip):
            scaled = jnp.concatenate(
                [(forms[q] * radial[q, p, j : j + 1, :]).astype(BF16) for q in range(group)], axis=0
            )
            block = lax.dot_general(strip[j], scaled, NT, preferred_element_type=F32)
            results[p, j * nmom : (j + 1) * nmom, :] = block.astype(BF16)
        send(p).start()
        return carry

    send(nrow).start()
    send(nrow + 1).start()
    lax.fori_loop(0, nrow, one, 0)
    for p in range(nrow + 2):
        send(p).wait()


def upper_kernel(own, slot, got, blocks, upper, low1, low2, spread, chosen, low_sems):
    npiv, half = chosen.shape
    ndev, rows, lanes = got.shape[0], spread.shape[0] // got.shape[0], got.shape[2]
    wide = blocks.shape[2]
    lows = []
    for i, low in enumerate((low1, low2)):
        for h in range(npiv // wide):
            lows.append(
                pltpu.make_async_copy(
                    blocks.at[slot + i, pl.ds(h * npiv, npiv), :], low.at[:, pl.ds(h * wide, wide)], low_sems.at[i, h]
                )
            )
    for load in lows:
        load.start()
    spread[...] = got[:, got.shape[1] - rows :, :].astype(F32).reshape(ndev * rows, lanes)
    for g in range(half // lanes):
        for a in range(own):
            chosen[a * ndev : (a + 1) * ndev, g * lanes : (g + 1) * lanes] = spread[
                pl.ds(g * own + a, ndev, stride=rows), :
            ].astype(BF16)
    for load in lows:
        load.wait()
    for at in range(0, half, wide):
        rows_of = chosen[:, at : at + wide]
        part = jnp.dot(low1[...], rows_of, preferred_element_type=F32) + jnp.dot(
            low2[...], rows_of, preferred_element_type=F32
        )
        upper[at : at + wide, :] = part.T.astype(BF16)


def fetch_kernel(blocks, upper, out, sems):
    del upper
    loads = [pltpu.make_async_copy(blocks.at[p], out.at[p], sems.at[p]) for p in range(out.shape[0])]
    for load in loads:
        load.start()
    for load in loads:
        load.wait()


def update_kernel(deep, got, mine, theirs, before, out, upper_t, upper_all):
    nrow, scols, wide = before.shape
    half, npiv = mine.shape
    ncol = npiv // deep
    core = lax.rem(lax.axis_index("row"), CORES)
    upper_all[pl.ds(pl.multiple_of(core * half, half), half), :] = mine[...]
    upper_all[pl.ds(pl.multiple_of((1 - core) * half, half), half), :] = theirs[...]
    width = upper_t.shape[0]
    upper_t[...] = upper_all[pl.ds(pl.multiple_of(lax.axis_index("col") * width, width), width), :]
    for p in range(nrow):
        pieces = [
            got[p * ncol : (p + 1) * ncol, b * deep : (b + 1) * deep, :].reshape(npiv, LANES)
            for b in range(wide // LANES)
        ]
        columns = jnp.concatenate(pieces, axis=1)
        for upper, side in ((mine, core), (theirs, 1 - core)):
            span = pl.ds(pl.multiple_of(side * half, half), half)
            change = jnp.dot(upper[...], columns, preferred_element_type=F32)
            out[p, span, :] = (before[p, span, :].astype(F32) - change).astype(BF16)


def widen_kernel(got, out, broad, sent):
    ndev, width, wide = got.shape
    steps = sent.shape[0]
    many = ndev // steps
    sends = []
    for s in range(steps):
        for b in range(s * many, (s + 1) * many):
            broad[:, b * wide : (b + 1) * wide] = got[b].astype(F32)
        span = pl.ds(s * many * wide, many * wide)
        send = pltpu.make_async_copy(broad.at[:, span], out.at[:, span], sent.at[s])
        send.start()
        sends.append(send)
    for send in sends:
        send.wait()


def shards(
    form_rows,
    form_strip,
    lam_index,
    coef_index,
    term_count,
    angular_coef,
    kernels,
    pivots,
    lower_inverse,
    panel,
):
    nrow = lax.axis_size("row")
    ncol = lax.axis_size("col")
    ndev = nrow * ncol
    chans, nmom, nrad = form_rows.shape
    nstrip, terms = lam_index.shape[1:]
    nlam = kernels.shape[0]
    npiv = pivots.shape[0]
    scols = nstrip * nmom
    width = scols // ncol
    own = npiv // ndev
    group = chans // nrow
    local = chans * nmom
    vmem = pl.BlockSpec(memory_space=pltpu.VMEM)
    anywhere = pl.BlockSpec(memory_space=pl.ANY)
    dma = pltpu.SemaphoreType.DMA

    tall = nmom // (CORES * CORES)
    extra = 2 * nstrip * terms
    deep1 = tall + own * (nrad + extra) // LANES
    steps, groups = 4, 4
    first = pl.pallas_call(
        functools.partial(pick_kernel, own),
        out_shape=jax.ShapeDtypeStruct((ndev, deep1, LANES), BF16),
        in_specs=[anywhere] * 6,
        out_specs=anywhere,
        scratch_shapes=[
            pltpu.VMEM((1, npiv), jnp.int32),
            pltpu.VMEM((nstrip * terms, chans), jnp.int32),
            pltpu.VMEM((nstrip * terms, chans), jnp.int32),
            pltpu.VMEM((nstrip, chans), jnp.int32),
            pltpu.VMEM(form_strip.shape, BF16),
            pltpu.VMEM((npiv, nrad + extra), F32),
            pltpu.VMEM((steps, local // steps, nrad), BF16),
            pltpu.VMEM((ndev, deep1, LANES), BF16),
            dma((5,)),
            dma((steps,)),
            dma((groups,)),
        ],
        compiler_params=room(56),
        cost_estimate=cost(2 * npiv * local * nrad, 4 << 20),
        name="pick_pivots",
    )(
        pivots[None, :],
        lam_index.transpose(1, 2, 0).reshape(nstrip * terms, chans),
        coef_index.transpose(1, 2, 0).reshape(nstrip * terms, chans),
        term_count.T,
        form_rows.reshape(local, nrad),
        form_strip,
    )
    deep, wide = panel.shape[0], panel.shape[1] // ndev
    flat = deep * wide // LANES
    cut = panel.reshape(deep, ndev, wide // LANES, LANES).transpose(1, 2, 0, 3).reshape(ndev, flat, LANES)
    half = scols // CORES
    wave_rows = own * half // LANES
    second = jnp.pad(cut, ((0, 0), (0, wave_rows), (0, 0)))
    got = exchange(first)
    got, second = lax.optimization_barrier((got, second))
    other = lax.ppermute(got, "row", [(i, i ^ 1) for i in range(nrow)])

    many = 32
    scaled = pl.pallas_call(
        functools.partial(scale_kernel, own, nstrip),
        out_shape=jax.ShapeDtypeStruct((own * nstrip, nrad), BF16),
        in_specs=[anywhere] * 3,
        out_specs=vmem,
        scratch_shapes=[
            pltpu.VMEM((ndev, deep1 - tall, LANES), BF16),
            pltpu.VMEM(kernels.shape, F32),
            pltpu.VMEM((angular_coef.shape[0], 1), F32),
            dma((3,)),
        ],
        compiler_params=room(40),
        cost_estimate=cost(2 * own * nstrip * nrad * LANES, 1 << 20),
        name="scale_pivots",
    )(got, kernels, angular_coef[:, None])
    second = pl.pallas_call(
        functools.partial(chosen_kernel, own),
        out_shape=jax.ShapeDtypeStruct(second.shape, BF16),
        in_specs=[anywhere, anywhere, vmem, anywhere],
        out_specs=anywhere,
        scratch_shapes=[
            pltpu.VMEM((nstrip, nmom, nrad), BF16),
            pltpu.VMEM((many, wave_rows, LANES), BF16),
            dma((CORES * nrow,)),
            dma((ndev // many,)),
        ],
        input_output_aliases={3: 0},
        compiler_params=room(40),
        cost_estimate=cost(2 * own * nstrip * scols * nrad, 4 << 20),
        name="chosen_rows",
    )(got, other, scaled, second)
    got2 = exchange(second)

    position = lax.broadcasted_iota(jnp.int32, lam_index.shape, 2)
    lam = jnp.where(position < term_count[:, :, None], lam_index, nlam)
    mixing = mixing_weights(lam, coef_index, angular_coef, nlam)
    radial = weights_to_radial(mixing, kernels)
    lower = lower_inverse.reshape(npiv, ndev, own).transpose(0, 2, 1).reshape(npiv, npiv)
    slots = 10 * nrow
    blocks = pl.pallas_call(
        assemble_kernel,
        out_shape=jax.ShapeDtypeStruct((slots, scols, group * nmom), BF16),
        in_specs=[vmem, vmem, anywhere, anywhere, vmem],
        out_specs=anywhere,
        scratch_shapes=[
            pltpu.VMEM((nstrip, nmom, nrad), BF16),
            pltpu.VMEM((nrow + 2, scols, group * nmom), BF16),
            dma((CORES * nrow,)),
            dma((nrow + 2,)),
        ],
        compiler_params=room(56),
        cost_estimate=cost(2 * local * scols * nrad * 4, 8 << 20),
        name="assemble_strip",
    )(form_rows.reshape(group, nrow, nmom, nrad), radial.reshape(group, nrow, nstrip, nrad), got, other, lower)

    mine = pl.pallas_call(
        functools.partial(upper_kernel, own, nrow),
        out_shape=jax.ShapeDtypeStruct((half, npiv), BF16),
        in_specs=[vmem, anywhere],
        out_specs=vmem,
        scratch_shapes=[
            pltpu.VMEM((npiv, npiv), BF16),
            pltpu.VMEM((npiv, npiv), BF16),
            pltpu.VMEM((ndev * wave_rows, LANES), F32),
            pltpu.VMEM((npiv, half), BF16),
            dma((2, npiv // wide)),
        ],
        compiler_params=room(24),
        cost_estimate=cost(4 * npiv * npiv * half, 2 << 20),
        name="upper_rows",
    )(got2, blocks)
    theirs = lax.ppermute(mine, "row", [(i, i ^ 1) for i in range(nrow)])
    fetched = pl.pallas_call(
        fetch_kernel,
        out_shape=jax.ShapeDtypeStruct((nrow, scols, wide), BF16),
        in_specs=[anywhere, anywhere],
        out_specs=vmem,
        scratch_shapes=[dma((nrow,))],
        compiler_params=room(16),
        cost_estimate=cost(0, 8 << 20),
        name="fetch_blocks",
    )(blocks, mine)
    done, upper_t = pl.pallas_call(
        functools.partial(update_kernel, deep),
        out_shape=(
            jax.ShapeDtypeStruct((nrow, scols, wide), BF16),
            jax.ShapeDtypeStruct((width, npiv), BF16),
        ),
        in_specs=[vmem, vmem, vmem, vmem],
        out_specs=(vmem, vmem),
        scratch_shapes=[pltpu.VMEM((scols, npiv), BF16)],
        compiler_params=room(16),
        cost_estimate=cost(2 * npiv * scols * local, 12 << 20),
        name="update_blocks",
    )(got2, mine, theirs, fetched)
    final = exchange(done.reshape(ndev, width, wide))
    steps = 16
    trailing = pl.pallas_call(
        widen_kernel,
        out_shape=jax.ShapeDtypeStruct((width, ndev * wide), F32),
        in_specs=[vmem],
        out_specs=anywhere,
        scratch_shapes=[pltpu.VMEM((width, ndev * wide), F32), dma((steps,))],
        compiler_params=room(20),
        cost_estimate=cost(ndev * width * wide, 12 << 20),
        name="widen_blocks",
    )(final)
    return (trailing, upper_t)


def solution(mesh):
    in_specs = (
        P(("row", "col"), None, None),
        P("col", None, None),
        P(("row", "col"), None, None),
        P(("row", "col"), None, None),
        P(("row", "col"), None),
        P(),
        P(),
        P(),
        P(),
        P("col", "row"),
    )
    out_specs = (P("col", "row"), P("col", None))
    return jax.shard_map(shards, mesh=mesh, in_specs=in_specs, out_specs=out_specs, check_vma=False)
```
